128 devices in a mesh: node: 16 (over z_hi, y, core), local: 8 (over x, z_lo).
Axes of the slice: x: 4, y: 4, z: 4 (z_hi: 2, z_lo: 2; z = z_hi * 2 + z_lo), core: 2. Of those that a mesh axis runs over, the one named last changes fastest.
Arguments:
- tokens: bfloat16 [16384, 2048], P(('node', 'local')), may hold values from -6 to 6
- out_grad: bfloat16 [16384, 2048], P(('node', 'local')), may hold values from -6 to 6
- expert_ids: int32 [16384, 8], P(('node', 'local')), may hold values from 0 to 127, all different within a row; in each aligned block of 128 rows (0 to 127, 128 to 255, ...) at most 9 rows name the same one
- gates: bfloat16 [16384, 8], P(('node', 'local')), may hold values from 0.019897461 to 0.3984375
- gate_weight: bfloat16 [128, 2048, 768], P(('node', 'local')), may hold values from -0.125 to 0.125
- up_weight: bfloat16 [128, 2048, 768], P(('node', 'local')), may hold values from -0.125 to 0.125
- down_weight: bfloat16 [128, 768, 2048], P(('node', 'local')), may hold values from -0.21875 to 0.21875
Outputs:
- input_grad: bfloat16 [16384, 2048], P(('node', 'local'))
- gate_weight_grad: bfloat16 [128, 2048, 768], P(('node', 'local'))
- up_weight_grad: bfloat16 [128, 2048, 768], P(('node', 'local'))
- down_weight_grad: bfloat16 [128, 768, 2048], P(('node', 'local'))
The draws below stay inside these ranges and needn't reach their ends.
Inputs may be any that keep to these rules, and one draw needn't show every extreme that they name: `expert_ids`: each row names 8 different experts. Among the tokens of one device no expert is named more than 9 times, and in every draw some expert is named exactly 9 times by the tokens of some device.
All inputs are finite; a program needn't handle non-finite values.
Results may differ from the reference program's by a relative error of at most 0.0065.
Values may be sent and summed in bfloat16 or wider, within the bound.
A program may use at most 192 MiB of HBM per device.

```python
import math
import jax
import jax.numpy as jnp
import numpy as np
from jax import lax

D = 2048
FF = 768
TOP = 8
TOK_DEV = 128
EXPERTS = 128
TOKENS = 16384
CAP = 9


def steps_of(rng, dims, pieces, least, largest):
    def one(position, blocks):
        draws = jax.random.uniform(jax.random.fold_in(jax.random.fold_in(rng, 6), position), (blocks,), jnp.float32, least / len(pieces), largest / len(pieces))
        return jnp.repeat(jnp.exp(draws), dims[position] // blocks).reshape((-1,) + (1,) * (len(dims) - position - 1))

    factor_of = one(*pieces[0])
    for cut in pieces[1:]:
        factor_of = factor_of * one(*cut)
    return factor_of


def assign_block(key, own, number, rows, number_of, top, limit, lean):
    order = jax.random.permutation(key, number_of)
    crowded, ordinary = shares(number_of, rows * top, limit, lean, True), shares(number_of, rows * top, limit, lean, False)
    places = jnp.arange(number_of)

    def named(tallies, rotation):
        used = int((tallies > 0).sum())
        fixed = max(1, used // 4)
        moved = fixed + (places - fixed + rotation * (used - fixed)) % max(1, number_of - fixed)
        return jnp.zeros((number_of,), jnp.int32).at[order[jnp.where(places < fixed, places, moved)]].set(jnp.asarray(tallies, jnp.int32))

    tallies = jnp.where(number % 4 == 0, named(crowded, number // 4), named(ordinary, number - number // 4 - 1))
    mixed = jax.random.permutation(jax.random.fold_in(own, 3), number_of)
    donor, sink = mixed[0:number_of // 2 * 2:2], mixed[1:number_of // 2 * 2:2]
    margin = jnp.minimum(tallies[donor] - 1, limit - tallies[sink]) // 2
    margin = jnp.where((donor == order[0]) | (sink == order[0]) | (tallies[sink] == 0), 0, jnp.maximum(margin, 0))
    moved = jax.random.randint(jax.random.fold_in(own, 4), (number_of // 2,), 0, 1 << 20) % (margin + 1)
    tallies = tallies.at[donor].add(-moved).at[sink].add(moved)
    labels = jnp.searchsorted(jnp.cumsum(tallies), jnp.arange(rows * top), side="right").astype(jnp.int32)
    listing = labels.reshape(top, rows).T
    listing = listing[jax.random.permutation(jax.random.fold_in(own, 1), rows)]
    rotation = jax.random.randint(jax.random.fold_in(own, 2), (rows, 1), 0, top)
    return jnp.take_along_axis(listing, (jnp.arange(top)[None, :] + rotation) % top, axis=1)


def shares(number_of, total, limit, lean, full):
    weights = [(1 << 20) // math.isqrt(rank ** lean) + 1 for rank in range(1, number_of + 1)]
    largest = limit if full else min(limit, max(-(-total // number_of), total * weights[0] // sum(weights)))
    least = 1 if total - largest >= number_of - 1 else 0
    holding, rest = [largest] + [least] * (number_of - 1), total - largest - least * (number_of - 1)
    while rest > 0:
        candidates = [i for i in range(1, number_of) if holding[i] < largest] or [i for i in range(1, number_of) if holding[i] < limit]
        pool, remaining = sum([weights[i] for i in candidates]), rest
        for i in candidates:
            extra = min(limit - holding[i], max(1, remaining * weights[i] // pool), rest)
            holding[i] = holding[i] + extra
            rest = rest - extra
    return np.array(holding)


def noise(stream_key, extent, deviation, limit, cuts=(), kind=jnp.bfloat16):
    level = steps_of(stream_key, extent, cuts, -0.22, 0.18) if cuts else 1.0
    array = jax.random.normal(stream_key, extent, jnp.float32) * deviation * level
    return jnp.minimum(jnp.maximum(array, -limit), limit).astype(kind)


def setup_inputs(seed: int = 0) -> dict:
    keys = jax.random.split(jax.random.key(seed), 8)
    tokens = noise(keys[0], (TOKENS, D), 1.0, 6.0, ((0, 128),))
    out_grad = noise(keys[1], (TOKENS, D), 1.0, 6.0, ((0, 128),))
    expert_ids_keys = jax.random.split(jax.random.fold_in(keys[2], 1), TOKENS // TOK_DEV)
    expert_ids_turns = jax.random.permutation(jax.random.fold_in(keys[2], 3), TOKENS // TOK_DEV)
    expert_ids = jax.vmap(lambda own, number: assign_block(jax.random.fold_in(keys[2], 2), own, number, TOK_DEV, EXPERTS, TOP, CAP, 1))(expert_ids_keys, expert_ids_turns).reshape((TOKENS, TOP))
    gates = jnp.clip(jnp.exp(math.log(0.3984375) - 2.9969585 * jax.random.uniform(keys[3], (TOKENS, TOP), jnp.float32) ** steps_of(keys[3], (TOKENS, TOP), ((0, 128),), -0.2, 0.2)), 0.019897461, 0.3984375).astype(jnp.bfloat16)
    gate_weight = noise(keys[4], (EXPERTS, D, FF), D ** -0.5, 0.125, ((0, 128),))
    up_weight = noise(keys[5], (EXPERTS, D, FF), D ** -0.5, 0.125, ((0, 128),))
    down_weight = noise(keys[6], (EXPERTS, FF, D), FF ** -0.5, 0.21875, ((0, 128),))
    return {"tokens": tokens, "out_grad": out_grad, "expert_ids": expert_ids, "gates": gates, "gate_weight": gate_weight, "up_weight": up_weight, "down_weight": down_weight}


def slot_table(expert_ids, blocks, experts, slot_cap):
    pair_ids = expert_ids.reshape(blocks, -1).astype(jnp.int32)
    per_block = pair_ids.shape[1]
    onehot = (pair_ids[:, :, None] == jnp.arange(experts, dtype=jnp.int32)[None, None, :]).astype(jnp.int32)
    earlier = (jnp.cumsum(onehot, axis=1) - onehot).astype(jnp.int32)
    slot_index = jnp.sum(earlier * onehot, axis=2).astype(jnp.int32)
    sources = jnp.arange(blocks, dtype=jnp.int32)[:, None]
    positions = pair_ids * (blocks * slot_cap) + sources * slot_cap + slot_index
    pair_global = jnp.arange(blocks * per_block, dtype=jnp.int32)
    owners = jnp.full((experts * blocks * slot_cap,), blocks * per_block, jnp.int32)
    owners = owners.at[positions.reshape(-1)].set(pair_global)
    return owners.reshape(experts, blocks * slot_cap)


def reference(tokens, out_grad, expert_ids, gates, gate_weight, up_weight, down_weight):
    blocks = TOKENS // TOK_DEV
    owners = slot_table(expert_ids, blocks, EXPERTS, CAP)
    zero_row = jnp.zeros((1, D), tokens.dtype)
    token_pad = jnp.concatenate([tokens, zero_row], axis=0)
    grad_pad = jnp.concatenate([out_grad, zero_row], axis=0)
    gate_pad = jnp.concatenate([gates.reshape(-1), jnp.zeros((1,), gates.dtype)], axis=0)

    def one_expert(operands):
        owner_row, gate_matrix, up_matrix, down_matrix = operands
        token_index = owner_row // TOP
        expert_input = token_pad[token_index]
        expert_grad = (gate_pad[owner_row].astype(jnp.float32)[:, None]
                       * grad_pad[token_index].astype(jnp.float32)).astype(jnp.bfloat16)
        gate_pre = jnp.dot(expert_input, gate_matrix, preferred_element_type=jnp.float32)
        up_pre = jnp.dot(expert_input, up_matrix, preferred_element_type=jnp.float32)
        logistic = jax.nn.sigmoid(gate_pre)
        silu_gate = gate_pre * logistic
        hidden = (silu_gate * up_pre).astype(jnp.bfloat16)
        hidden_grad = jnp.dot(expert_grad, down_matrix.T, preferred_element_type=jnp.float32)
        up_grad = (hidden_grad * silu_gate).astype(jnp.bfloat16)
        gate_grad = (hidden_grad * up_pre * logistic * (1.0 + gate_pre * (1.0 - logistic))).astype(jnp.bfloat16)
        down_out = jnp.dot(hidden.T, expert_grad, preferred_element_type=jnp.float32).astype(jnp.bfloat16)
        gate_out = jnp.dot(expert_input.T, gate_grad, preferred_element_type=jnp.float32).astype(jnp.bfloat16)
        up_out = jnp.dot(expert_input.T, up_grad, preferred_element_type=jnp.float32).astype(jnp.bfloat16)
        slot_grad = (jnp.dot(gate_grad, gate_matrix.T, preferred_element_type=jnp.float32)
                     + jnp.dot(up_grad, up_matrix.T, preferred_element_type=jnp.float32)).astype(jnp.bfloat16)
        return slot_grad, gate_out, up_out, down_out

    slot_grad, gate_weight_grad, up_weight_grad, down_weight_grad = lax.map(
        one_expert, (owners, gate_weight, up_weight, down_weight))
    pair_rows = jnp.zeros((TOKENS * TOP + 1, D), slot_grad.dtype)
    pair_rows = pair_rows.at[owners.reshape(-1)].set(slot_grad.reshape(-1, D))
    summed = jnp.sum(pair_rows[:-1].reshape(TOKENS, TOP, D).astype(jnp.float32), axis=1)
    input_grad = summed.astype(jnp.bfloat16)
    return input_grad, gate_weight_grad, up_weight_grad, down_weight_grad
```

```python
import functools

import jax
import jax.numpy as jnp
from jax import lax
from jax.experimental import pallas as pl
from jax.experimental.pallas import tpu as pltpu
from jax.sharding import PartitionSpec as P

MESH = pl.DeviceIdType.MESH
BF, F32 = jnp.bfloat16, jnp.float32
D, FF, TOK, TOP, SLOTS = 2048, 768, 128, 8, 9
WIDTH = (640, 768, 640)
START = (0, 640, 1408)
HALF = 384
ROWS = 1152


def place():
    node, local = lax.axis_index("node"), lax.axis_index("local")
    return local // 2, (node % 8) // 2, (node // 8) * 2 + local % 2, node % 2


def order(j, x, y, z):
    return ((x, y, z), (y, z, x), (z, x, y))[j]


def device(j, a, b, c, core):
    x, y, z = ((a, b, c), (c, a, b), (b, c, a))[j]
    return ((z // 2) * 8 + y * 2 + core, x * 2 + z % 2)


def canon(j, ref, b, c, lead, cols):
    if j == 0:
        place_of = (c, b, slice(None))
    elif j == 1:
        place_of = (b, slice(None), c)
    else:
        place_of = (slice(None), c, b)
    return ref.at[lead + place_of + (slice(None), cols)]


def remote(src, dst, ssem, rsem, dev):
    return pltpu.make_async_remote_copy(
        src_ref=src, dst_ref=dst, send_sem=ssem, recv_sem=rsem, device_id=dev, device_id_type=MESH
    )


def greet(partners):
    barrier = pltpu.get_barrier_semaphore()
    for dev in partners:
        pl.semaphore_signal(barrier, inc=1, device_id=dev, device_id_type=MESH)
    pl.semaphore_wait(barrier, len(partners))


def partners_of(x, y, z, core):
    out = [device(0, x, y, z, 1 - core)]
    for d in (1, 2, 3):
        out.append(device(0, (x + d) % 4, y, z, core))
        out.append(device(0, x, (y + d) % 4, z, core))
        out.append(device(0, x, y, (z + d) % 4, core))
    return out


def iota(shape, dim):
    return lax.broadcasted_iota(jnp.int32, shape, dim)


def tail_perm(j, array):
    row, col = iota((128, 256), 0), iota((128, 256), 1)
    core, x, y, z = row % 2, (row // 2) % 4, (row // 8) % 4, row // 32
    a, b, c = order(j, x, y, z)
    want = c * 64 + b * 16 + array * 8 + a * 2 + core
    return (col == want).astype(F32).astype(BF)


def dispatch_kernel(tok, grad, meta, xg, xg_tail, pos_out, *scr):
    T, S, ST, R, RT, FT = (scr[3 * i : 3 * i + 3] for i in range(6))
    (metas, ag_s, ag_r, sib_s, sib_r, mag_s, mag_r, msib_s, msib_r, p2_s, p2_r, p2t_s, p2t_r,
     p3_s, p3_r, p3t_s, p3t_r, loc, locm, locp, loct, outs) = scr[18:]
    x, y, z, core = place()
    greet(partners_of(x, y, z, core))
    sib = device(0, x, y, z, 1 - core)
    ins = (tok, grad)
    sends = []

    def go(cp):
        cp.start()
        sends.append(cp)

    for j in range(3):
        a, b, c = order(j, x, y, z)
        cols = pl.ds(START[j], WIDTH[j])
        for d in (2, 1, 3):
            dev = device(j, (a + d) % 4, b, c, core)
            go(remote(meta, metas.at[j, a, core], mag_s.at[j, d], mag_r.at[j, a], dev))
        for d in (2, 1, 3):
            dev = device(j, (a + d) % 4, b, c, core)
            for r in range(2):
                go(remote(ins[r].at[:, cols], T[j].at[r, a, core], ag_s.at[j, d, r], ag_r.at[j, a, r], dev))
    for j in range(3):
        a, b, c = order(j, x, y, z)
        cols = pl.ds(START[j], WIDTH[j])
        go(remote(meta, metas.at[j, a, core], msib_s.at[j, a], msib_r.at[j, a], sib))
        pltpu.make_async_copy(meta, metas.at[j, a, core], locm.at[j]).start()
        for r in range(2):
            go(remote(ins[r].at[:, cols], T[j].at[r, a, core], sib_s.at[j, a, r], sib_r.at[j, a, r], sib))
            pltpu.make_async_copy(ins[r].at[:, cols], T[j].at[r, a, core], loc.at[j, r]).start()

    for d in (1, 3, 2):
        for j in range(3):
            a, b, c = order(j, x, y, z)
            s = (a + d) % 4
            m = metas.at[j, s, core]
            remote(m, m, mag_s.at[j, 0], mag_r.at[j, s], sib).wait_recv()
            go(remote(m, m, msib_s.at[j, s], msib_r.at[j, s], sib))
            for r in range(2):
                t = T[j].at[r, s, core]
                remote(t, t, ag_s.at[j, 0, r], ag_r.at[j, s, r], sib).wait_recv()
                go(remote(t, t, sib_s.at[j, s, r], sib_r.at[j, s, r], sib))

    before = (iota((TOK, TOK), 0) < iota((TOK, TOK), 1)).astype(F32).astype(BF)
    for j in range(3):
        a, b, c = order(j, x, y, z)
        w = WIDTH[j]
        e = iota((16, 1), 0)
        dev = device(j, a, e // 4, e % 4, core)
        expert = (dev[0] * 8 + dev[1]).astype(F32)
        pltpu.make_async_copy(meta, metas.at[j, a, core], locm.at[j]).wait()
        for r in range(2):
            pltpu.make_async_copy(ins[r].at[:, pl.ds(START[j], w)], T[j].at[r, a, core], loc.at[j, r]).wait()
        for s in range(4):
            m = metas.at[j, s, 1 - core]
            remote(m, m, msib_s.at[j, s], msib_r.at[j, s], sib).wait_recv()
            for r in range(2):
                t = T[j].at[r, s, 1 - core]
                remote(t, t, sib_s.at[j, s, r], sib_r.at[j, s, r], sib).wait_recv()
        tails = [jnp.zeros((128, w), F32), jnp.zeros((128, w), F32)]
        for s in range(4):
            pick, pick_tail = [[], []], [[], []]
            for k in range(2):
                info = metas[j, s, k]
                named = jnp.zeros((16, TOK), F32)
                gate = jnp.zeros((16, TOK), F32)
                for i in range(TOP):
                    hit = info[i : i + 1, :] == expert
                    named = named + jnp.where(hit, 1.0, 0.0)
                    gate = gate + jnp.where(hit, info[TOP + i : TOP + i + 1, :], 0.0)
                earlier = jnp.dot(named.astype(BF), before, preferred_element_type=F32)
                pos = jnp.where(named > 0.5, earlier, -1.0)
                pos_out[j, s, k] = pos
                target = (pos * 2.0 + k)[:, None, :]
                hit = target == iota((16, 16, TOK), 1).astype(F32)
                pick[0].append(jnp.where(hit, 1.0, 0.0).reshape(256, TOK))
                pick[1].append(jnp.where(hit, gate[:, None, :], 0.0).reshape(256, TOK))
                hit = (pos[:, None, :] == 8.0) & (iota((16, 8, TOK), 1) == 2 * s + k)
                pick_tail[0].append(jnp.where(hit, 1.0, 0.0).reshape(128, TOK))
                pick_tail[1].append(jnp.where(hit, gate[:, None, :], 0.0).reshape(128, TOK))
            for r in range(2):
                rows = T[j][r, s].reshape(2 * TOK, w)
                main = jnp.dot(jnp.concatenate(pick[r], axis=1).astype(BF), rows, preferred_element_type=F32)
                S[j][:, :, r, s] = main.astype(BF).reshape(4, 4, 16, w)
                tails[r] = tails[r] + jnp.dot(
                    jnp.concatenate(pick_tail[r], axis=1).astype(BF), rows, preferred_element_type=F32
                )
        both = jnp.concatenate([t.reshape(16, 8, w) for t in tails], axis=1)
        ST[j][...] = both.astype(BF).reshape(4, 4, 16, w)
        for d in (2, 1, 3):
            t = (b + d) % 4
            go(remote(S[j].at[t], R[j].at[b], p2_s.at[j, d], p2_r.at[j, b], device(j, a, t, c, core)))
            go(remote(ST[j].at[t], RT[j].at[b], p2t_s.at[j, d], p2t_r.at[j, b], device(j, a, t, c, core)))
        onward(j, a, b, c, core, b, 0, S, ST, xg, FT, go, p3_s, p3_r, p3t_s, p3t_r, locp, loct)

    for d in (1, 3, 2):
        for j in range(3):
            a, b, c = order(j, x, y, z)
            s = (b + d) % 4
            remote(R[j].at[s], R[j].at[s], p2_s.at[j, 0], p2_r.at[j, s], sib).wait_recv()
            remote(RT[j].at[s], RT[j].at[s], p2t_s.at[j, 0], p2t_r.at[j, s], sib).wait_recv()
            onward(j, a, b, c, core, s, d, R, RT, xg, FT, go, p3_s, p3_r, p3t_s, p3t_r, locp, loct)

    for j in range(3):
        a, b, c = order(j, x, y, z)
        cols = pl.ds(START[j], WIDTH[j])
        for db in range(4):
            sb = (b + db) % 4
            pltpu.make_async_copy(FT[j].at[c, sb], FT[j].at[c, sb], loct.at[j, db]).wait()
            for dc in (1, 2, 3):
                sc = (c + dc) % 4
                f = FT[j].at[sc, sb]
                remote(f, f, p3t_s.at[j, 0, 0], p3t_r.at[j, sc, sb], sib).wait_recv()
        rows = FT[j][...].reshape(256, WIDTH[j])
        for r in range(2):
            xg_tail[r, :, cols] = jnp.dot(tail_perm(j, r), rows, preferred_element_type=F32).astype(BF)
    for j in range(3):
        a, b, c = order(j, x, y, z)
        cols = pl.ds(START[j], WIDTH[j])
        for db in range(4):
            sb = (b + db) % 4
            f = canon(j, xg, sb, c, (slice(None),), cols)
            pltpu.make_async_copy(f, f, locp.at[j, db]).wait()
            for dc in (1, 2, 3):
                sc = (c + dc) % 4
                f = canon(j, xg, sb, sc, (slice(None),), cols)
                remote(f, f, p3_s.at[j, 0, 0], p3_r.at[j, sc, sb], sib).wait_recv()
    for cp in sends:
        cp.wait_send()


def onward(j, a, b, c, core, s, d, main, tail, xg, FT, go, p3_s, p3_r, p3t_s, p3t_r, locp, loct):
    cols = pl.ds(START[j], WIDTH[j])
    dst = canon(j, xg, s, c, (slice(None),), cols)
    for dc in (2, 1, 3):
        t = (c + dc) % 4
        dev = device(j, a, b, t, core)
        go(remote(main[j].at[s, t], dst, p3_s.at[j, d, dc], p3_r.at[j, c, s], dev))
        go(remote(tail[j].at[s, t], FT[j].at[c, s], p3t_s.at[j, d, dc], p3t_r.at[j, c, s], dev))
    pltpu.make_async_copy(main[j].at[s, c], dst, locp.at[j, d]).start()
    pltpu.make_async_copy(tail[j].at[s, c], FT[j].at[c, s], loct.at[j, d]).start()


def dispatch(tokens, out_grad, meta):
    dma = pltpu.SemaphoreType.DMA
    vm = pltpu.VMEM
    any_spec = pl.BlockSpec(memory_space=pl.ANY)
    scratch = [vm((2, 4, 2, TOK, w), BF) for w in WIDTH]
    for _ in range(2):
        scratch += [vm((4, 4, 2, 4, 16, w), BF) for w in WIDTH]
        scratch += [vm((4, 4, 16, w), BF) for w in WIDTH]
    scratch += [vm((4, 4, 16, w), BF) for w in WIDTH]
    scratch += [vm((3, 4, 2, 16, TOK), F32)]
    scratch += [dma((3, 4, 2))] * 4 + [dma((3, 4))] * 4 + [dma((3, 4))] * 4 + [dma((3, 4, 4))] * 4
    scratch += [dma((3, 2)), dma((3,)), dma((3, 4)), dma((3, 4)), dma]
    return pl.pallas_call(
        dispatch_kernel,
        name="dispatch",
        out_shape=(
            jax.ShapeDtypeStruct((2, 4, 4, 4, 16, D), BF),
            jax.ShapeDtypeStruct((2, 128, D), BF),
            jax.ShapeDtypeStruct((3, 4, 2, 16, TOK), F32),
        ),
        in_specs=[any_spec] * 3,
        out_specs=(any_spec, pl.BlockSpec(memory_space=pltpu.VMEM), pl.BlockSpec(memory_space=pltpu.VMEM)),
        scratch_shapes=scratch,
        compiler_params=pltpu.CompilerParams(collective_id=0, has_side_effects=True, vmem_limit_bytes=60 << 20),
    )(tokens, out_grad, meta)


def tail_spread(j, half):
    row, col = iota((256, 128), 0), iota((256, 128), 1)
    c, b, h, a, core = row // 64, (row // 16) % 4, (row // 8) % 2, (row // 2) % 4, row % 2
    x, y, z = ((a, b, c), (c, a, b), (b, c, a))[j]
    return ((col == z * 32 + y * 8 + x * 2 + core) & (h == half)).astype(F32).astype(BF)


def over_rows(left, right):
    return lax.dot_general(left, right, (((0,), (0,)), ((), ())), preferred_element_type=F32)


def collect_kernel(sg, sg_tail, pos, out, *scr):
    ST, R1, RT1, R2, RT2, PS, PR, QS, QR, KEEP = (scr[3 * i : 3 * i + 3] for i in range(10))
    (r1_s, r1_r, r1t_s, r1t_r, r2_s, r2_r, r2t_s, r2t_r, loc, loct, ps_s, ps_r, q_s, q_r) = scr[30:]
    x, y, z, core = place()
    greet(partners_of(x, y, z, core))
    sib = device(0, x, y, z, 1 - core)
    sends = []

    def go(cp):
        cp.start()
        sends.append(cp)

    def of_c(j, t):
        cols = pl.ds(START[j], WIDTH[j])
        if j == 0:
            return sg.at[t, :, :, :, cols]
        if j == 1:
            return sg.at[:, :, t, :, cols]
        return sg.at[:, t, :, :, cols]

    def of_b(j, ref, t):
        return ref.at[:, t] if j == 2 else ref.at[t]

    def spread(j, c_tiles, c_tails, s, A, B, C, d):
        for db in (2, 1, 3):
            t = (B + db) % 4
            dev = device(j, A, t, C, core)
            go(remote(c_tiles(t), R2[j].at[B, s], r2_s.at[j, d, db], r2_r.at[j, B, s], dev))
            go(remote(c_tails.at[t], RT2[j].at[B, s], r2t_s.at[j, d, db], r2t_r.at[j, B, s], dev))
        pltpu.make_async_copy(c_tiles(B), R2[j].at[B, s], loc.at[j, d]).start()
        pltpu.make_async_copy(c_tails.at[B], RT2[j].at[B, s], loct.at[j, d]).start()

    for d in (2, 1, 3):
        for j in range(3):
            A, B, C = order(j, x, y, z)
            t = (C + d) % 4
            go(remote(of_c(j, t), R1[j].at[C], r1_s.at[j, d], r1_r.at[j, C], device(j, A, B, t, core)))
    for j in range(3):
        A, B, C = order(j, x, y, z)
        lo, hi = START[j], START[j] + WIDTH[j] - HALF
        rows = jnp.dot(tail_spread(j, 0), sg_tail[:, lo : lo + HALF], preferred_element_type=F32)
        rows = rows + jnp.dot(tail_spread(j, 1), sg_tail[:, hi : hi + HALF], preferred_element_type=F32)
        ST[j][...] = rows.astype(BF).reshape(4, 4, 16, HALF)
        for d in (2, 1, 3):
            t = (C + d) % 4
            go(remote(ST[j].at[t], RT1[j].at[C], r1t_s.at[j, d], r1t_r.at[j, C], device(j, A, B, t, core)))
        spread(j, lambda t: canon(j, sg, t, C, (), pl.ds(START[j], WIDTH[j])), ST[j].at[C], C, A, B, C, 0)
    for d in (1, 3, 2):
        for j in range(3):
            A, B, C = order(j, x, y, z)
            s = (C + d) % 4
            remote(R1[j].at[s], R1[j].at[s], r1_s.at[j, 0], r1_r.at[j, s], sib).wait_recv()
            remote(RT1[j].at[s], RT1[j].at[s], r1t_s.at[j, 0], r1t_r.at[j, s], sib).wait_recv()
            spread(j, lambda t: of_b(j, R1[j].at[s], t), RT1[j].at[s], s, A, B, C, d)

    for j in range(3):
        A, B, C = order(j, x, y, z)
        w = WIDTH[j]
        for dc in range(4):
            s = (C + dc) % 4
            pltpu.make_async_copy(R2[j].at[B, s], R2[j].at[B, s], loc.at[j, dc]).wait()
            pltpu.make_async_copy(RT2[j].at[B, s], RT2[j].at[B, s], loct.at[j, dc]).wait()
            for db in (1, 2, 3):
                t = (B + db) % 4
                f = R2[j].at[t, s]
                remote(f, f, r2_s.at[j, 0, 0], r2_r.at[j, t, s], sib).wait_recv()
                f = RT2[j].at[t, s]
                remote(f, f, r2t_s.at[j, 0, 0], r2t_r.at[j, t, s], sib).wait_recv()
        for d in (2, 1, 3, 0):
            s = (A + d) % 4
            pick, low, high = [], [], []
            for k in range(2):
                who = (core + k) % 2
                at = pos[j, s, who]
                target = (at * 2.0 + who.astype(F32))[:, None, :]
                hit = target == iota((16, 16, TOK), 1).astype(F32)
                pick.append(jnp.where(hit, 1.0, 0.0).reshape(256, TOK))
                last = at[:, None, :] == 8.0
                row = iota((16, 16, TOK), 1)
                low.append(jnp.where(last & (row == 2 * s + who), 1.0, 0.0).reshape(256, TOK))
                high.append(jnp.where(last & (row == 8 + 2 * s + who), 1.0, 0.0).reshape(256, TOK))
            pick, low, high = (jnp.concatenate(p, axis=1).astype(BF) for p in (pick, low, high))
            tails = RT2[j][...].reshape(256, HALF)
            total = over_rows(pick, R2[j][:, :, s].reshape(256, w))
            total = total + jnp.concatenate(
                [over_rows(low, tails), over_rows(high, tails)[:, 2 * HALF - w :]], axis=1
            )
            KEEP[j][d] = total[:TOK]
            PS[j][d] = total[TOK:].astype(BF)
            go(remote(PS[j].at[d], PR[j].at[d], ps_s.at[j, d], ps_r.at[j, d], sib))
        for d in (2, 1, 3):
            s = (A + d) % 4
            remote(PR[j].at[d], PR[j].at[d], ps_s.at[j, 0], ps_r.at[j, d], sib).wait_recv()
            QS[j][d] = (KEEP[j][d] + PR[j][d].astype(F32)).astype(BF)
            go(remote(QS[j].at[d], QR[j].at[d], q_s.at[j, d], q_r.at[j, d], device(j, s, B, C, core)))
    for j in range(3):
        w = WIDTH[j]
        remote(PR[j].at[0], PR[j].at[0], ps_s.at[j, 0], ps_r.at[j, 0], sib).wait_recv()
        total = KEEP[j][0] + PR[j][0].astype(F32)
        for d in (1, 3, 2):
            remote(QR[j].at[d], QR[j].at[d], q_s.at[j, 0], q_r.at[j, d], sib).wait_recv()
            total = total + QR[j][d].astype(F32)
        out[:, START[j] : START[j] + w] = total.astype(BF)
    for cp in sends:
        cp.wait_send()


def collect(sg, sg_tail, pos):
    dma = pltpu.SemaphoreType.DMA
    vm = pltpu.VMEM
    any_spec = pl.BlockSpec(memory_space=pl.ANY)
    vm_spec = pl.BlockSpec(memory_space=pltpu.VMEM)
    scratch = [vm((4, 4, 16, HALF), BF) for w in WIDTH]
    for _ in range(2):
        scratch += [vm((4, 4, 4, 16, w), BF) for w in WIDTH]
        scratch += [vm((4, 4, 16, HALF), BF) for w in WIDTH]
    for kind in (BF, BF, BF, BF, F32):
        scratch += [vm((4, TOK, w), kind) for w in WIDTH]
    scratch += [dma((3, 4))] * 4 + [dma((3, 4, 4))] * 4 + [dma((3, 4))] * 6
    return pl.pallas_call(
        collect_kernel,
        name="collect",
        out_shape=jax.ShapeDtypeStruct((TOK, D), BF),
        in_specs=[any_spec, vm_spec, vm_spec],
        out_specs=vm_spec,
        scratch_shapes=scratch,
        compiler_params=pltpu.CompilerParams(collective_id=1, has_side_effects=True, vmem_limit_bytes=60 << 20),
    )(sg, sg_tail, pos)


def body(tokens, out_grad, expert_ids, gates, gate_weight, up_weight, down_weight):
    meta = jnp.concatenate([expert_ids.astype(F32), gates.astype(F32)], axis=1).T
    xg, xg_tail, pos = dispatch(tokens, out_grad, meta)
    main = xg.reshape(2, 1024, D)
    rows = jnp.concatenate([main[0], xg_tail[0]], axis=0)
    grads = jnp.concatenate([main[1], xg_tail[1]], axis=0)
    wg, wu, wd = gate_weight[0], up_weight[0], down_weight[0]

    def mm(spec, left, right):
        return jnp.einsum(spec, left, right, preferred_element_type=F32)

    gate_pre, up_pre = mm("rd,df->rf", rows, wg), mm("rd,df->rf", rows, wu)
    logistic = jax.nn.sigmoid(gate_pre)
    silu_gate = gate_pre * logistic
    hidden = (silu_gate * up_pre).astype(BF)
    hidden_grad = mm("rd,fd->rf", grads, wd)
    up_grad = (hidden_grad * silu_gate).astype(BF)
    gate_grad = (hidden_grad * up_pre * logistic * (1.0 + gate_pre * (1.0 - logistic))).astype(BF)
    slot_grad = (mm("rf,df->rd", gate_grad, wg) + mm("rf,df->rd", up_grad, wu)).astype(BF)
    input_grad = collect(slot_grad[:1024].reshape(4, 4, 4, 16, D), slot_grad[1024:], pos)
    down_weight_grad = mm("rf,rd->fd", hidden, grads).astype(BF)
    gate_weight_grad = mm("rd,rf->df", rows, gate_grad).astype(BF)
    up_weight_grad = mm("rd,rf->df", rows, up_grad).astype(BF)
    return input_grad, gate_weight_grad[None], up_weight_grad[None], down_weight_grad[None]


def solution(mesh):
    whole = ("node", "local")
    two, three = P(whole, None), P(whole, None, None)
    return jax.shard_map(
        body,
        mesh=mesh,
        in_specs=(two, two, two, two, three, three, three),
        out_specs=(two, three, three, three),
        check_vma=False,
    )
```

```python
import functools

import jax
import jax.numpy as jnp
from jax import lax
from jax.experimental import pallas as pl
from jax.experimental.pallas import tpu as pltpu
from jax.sharding import PartitionSpec as P

MESH = pl.DeviceIdType.MESH
BF, F32 = jnp.bfloat16, jnp.float32
D, FF, TOK, TOP, SLOTS = 2048, 768, 128, 8, 9
WIDTH = (640, 768, 640)
START = (0, 640, 1408)
HALF = 384
ROWS = 1152
MAIN_A, TAILS = 512, 128


def place():
    node, local = lax.axis_index("node"), lax.axis_index("local")
    return local // 2, (node % 8) // 2, (node // 8) * 2 + local % 2, node % 2


def order(j, x, y, z):
    return ((x, y, z), (y, z, x), (z, x, y))[j]


def device(j, a, b, c, core):
    x, y, z = ((a, b, c), (c, a, b), (b, c, a))[j]
    return ((z // 2) * 8 + y * 2 + core, x * 2 + z % 2)


def canon(j, ref, lead, par, b, c, cols):
    q = (par + b + c) % 2
    every = slice(None)
    if j == 0:
        at = (par, c // 2, c % 2, b // 2, b % 2, every)
    elif j == 1:
        at = (par, b // 2, b % 2, every, q, c // 2)
    else:
        at = (par, every, q, c // 2, c % 2, b // 2)
    return ref.at[lead + at + (every, cols)]


def remote(src, dst, ssem, rsem, dev):
    return pltpu.make_async_remote_copy(
        src_ref=src, dst_ref=dst, send_sem=ssem, recv_sem=rsem, device_id=dev, device_id_type=MESH
    )


def greet(partners):
    barrier = pltpu.get_barrier_semaphore()
    for dev in partners:
        pl.semaphore_signal(barrier, inc=1, device_id=dev, device_id_type=MESH)
    pl.semaphore_wait(barrier, len(partners))


def partners_of(x, y, z, core):
    out = [device(0, x, y, z, 1 - core)]
    for d in (1, 2, 3):
        out.append(device(0, (x + d) % 4, y, z, core))
        out.append(device(0, x, (y + d) % 4, z, core))
        out.append(device(0, x, y, (z + d) % 4, core))
    return out


def iota(shape, dim):
    return lax.broadcasted_iota(jnp.int32, shape, dim)


def tail_perm(j, array):
    row, col = iota((128, 256), 0), iota((128, 256), 1)
    core, x, y, z = row % 2, (row // 2) % 4, (row // 8) % 4, row // 32
    a, b, c = order(j, x, y, z)
    want = c * 64 + b * 16 + array * 8 + a * 2 + core
    return (col == want).astype(F32).astype(BF)


def tail_spread(j, half):
    row, col = iota((256, 128), 0), iota((256, 128), 1)
    c, b, h, a, core = row // 64, (row // 16) % 4, (row // 8) % 2, (row // 2) % 4, row % 2
    x, y, z = ((a, b, c), (c, a, b), (b, c, a))[j]
    return ((col == z * 32 + y * 8 + x * 2 + core) & (h == half)).astype(F32).astype(BF)


def over_rows(left, right):
    return lax.dot_general(left, right, (((0,), (0,)), ((), ())), preferred_element_type=F32)


def across(left, right):
    return lax.dot_general(left, right, (((1,), (1,)), ((), ())), preferred_element_type=F32)


def tile(i):
    return pl.ds(pl.multiple_of(i * 256, 256), 256)


def kernel(tok, grad, meta, gate_w, up_w, down_w, out, gate_out, up_out, down_out, *rest):
    (R, RT, R1, RT1), scr = (rest[3 * i : 3 * i + 3] for i in range(4)), rest[12:]
    T, S, ST, FT, ST2, R2, RT2, KEEP, OWN = (scr[3 * i : 3 * i + 3] for i in range(9))
    XG, XT, SG, SGT, WG, WU, WD, HID, GG, UG, metas, pos = scr[27:39]
    (ag_s, ag_r, sib_s, sib_r, mag_s, mag_r, msib_s, msib_r, loc, locm,
     p2_s, p2_r, p2t_s, p2t_r, p3_s, p3_r, p3t_s, p3t_r, locp, loct,
     r1_s, r1_r, r1t_s, r1t_r, r2_s, r2_r, r2t_s, r2t_r, l2, l2t,
     ps_s, ps_r, q_s, q_r, wsem, osem, done) = scr[39:]
    x, y, z, core = place()
    axes = [order(j, x, y, z) for j in range(3)]
    sib = device(0, x, y, z, 1 - core)
    weights = ((gate_w, WG), (up_w, WU), (down_w, WD))
    for i, (src, dst) in enumerate(weights):
        pltpu.make_async_copy(src.at[0], dst, wsem.at[i]).start()
    greet(partners_of(x, y, z, core))
    ins = (tok, grad)
    sends, early = [], []

    def go(cp, kept=sends):
        cp.start()
        kept.append(cp)

    def got(ref, rsem):
        remote(ref, ref, ag_s.at[0, 0, 0], rsem, sib).wait_recv()

    def landed(ref, sem):
        pltpu.make_async_copy(ref, ref, sem).wait()

    def cols_of(j):
        return pl.ds(START[j], WIDTH[j])

    for j in range(3):
        a, b, c = axes[j]
        for d in (2, 1, 3):
            dev = device(j, (a + d) % 4, b, c, core)
            go(remote(meta, metas.at[j, a, core], mag_s.at[j, d], mag_r.at[j, a], dev))
    for d in (2, 1, 3):
        for j in range(3):
            a, b, c = axes[j]
            dev = device(j, (a + d) % 4, b, c, core)
            for r in range(2):
                src = ins[r].at[:, cols_of(j)]
                go(remote(src, T[j].at[r, a, core], ag_s.at[j, d, r], ag_r.at[j, a, r], dev))
    for j in range(3):
        a, b, c = axes[j]
        go(remote(meta, metas.at[j, a, core], msib_s.at[j, a], msib_r.at[j, a], sib))
        pltpu.make_async_copy(meta, metas.at[j, a, core], locm.at[j]).start()
        for r in range(2):
            src = ins[r].at[:, cols_of(j)]
            go(remote(src, T[j].at[r, a, core], sib_s.at[j, a, r], sib_r.at[j, a, r], sib))
            pltpu.make_async_copy(src, T[j].at[r, a, core], loc.at[j, r]).start()

    for d in (1, 3, 2):
        for j in range(3):
            s = (axes[j][0] + d) % 4
            m = metas.at[j, s, core]
            got(m, mag_r.at[j, s])
            go(remote(m, m, msib_s.at[j, s], msib_r.at[j, s], sib))
        for j in range(3):
            s = (axes[j][0] + d) % 4
            for r in range(2):
                t = T[j].at[r, s, core]
                got(t, ag_r.at[j, s, r])
                go(remote(t, t, sib_s.at[j, s, r], sib_r.at[j, s, r], sib), early)

    before = (iota((TOK, TOK), 0) < iota((TOK, TOK), 1)).astype(F32).astype(BF)

    def one_hot(j, s, gate, last):
        a = axes[j][0]
        e = iota((16, 1), 0)
        dev = device(j, a, e // 4, e % 4, core)
        expert = (dev[0] * 8 + dev[1]).astype(F32)
        parts = []
        for k in range(2):
            info = metas[j, s, k]
            value = jnp.ones((16, TOK), F32)
            if gate:
                value = jnp.zeros((16, TOK), F32)
                for i in range(TOP):
                    hit = info[i : i + 1, :] == expert
                    value = value + jnp.where(hit, info[TOP + i : TOP + i + 1, :], 0.0)
            at = pos[j, s, k][:, None, :]
            if last:
                hit = (at == 8.0) & (iota((16, 8, TOK), 1) == 2 * s + k)
            else:
                hit = at * 2.0 + k == iota((16, 16, TOK), 1).astype(F32)
            parts.append(jnp.where(hit, value[:, None, :], 0.0).reshape(128 if last else 256, TOK))
        return jnp.concatenate(parts, axis=1).astype(BF)

    def find_slots(j):
        a = axes[j][0]
        e = iota((16, 1), 0)
        dev = device(j, a, e // 4, e % 4, core)
        expert = (dev[0] * 8 + dev[1]).astype(F32)
        for s in range(4):
            for k in range(2):
                info = metas[j, s, k]
                named = jnp.zeros((16, TOK), F32)
                for i in range(TOP):
                    named = named + jnp.where(info[i : i + 1, :] == expert, 1.0, 0.0)
                earlier = jnp.dot(named.astype(BF), before, preferred_element_type=F32)
                pos[j, s, k] = jnp.where(named > 0.5, earlier, -1.0)

    def gather(j, par):
        a, b, c = axes[j]
        w = WIDTH[j]
        for h in range(2):
            s = 2 * h + (par + b + c) % 2
            for r in range(2):
                rows = T[j][r, s].reshape(2 * TOK, w)
                main = jnp.dot(one_hot(j, s, r == 1, False), rows, preferred_element_type=F32)
                S[j][:, :, r, par, h] = main.astype(BF).reshape(4, 4, 16, w)

    def gather_tails(j):
        w = WIDTH[j]
        tails = []
        for r in range(2):
            rows = jnp.zeros((TAILS, w), F32)
            for s in range(4):
                picked = T[j][r, s].reshape(2 * TOK, w)
                rows = rows + jnp.dot(one_hot(j, s, r == 1, True), picked, preferred_element_type=F32)
            tails.append(rows.reshape(16, 8, w))
        ST[j][...] = jnp.concatenate(tails, axis=1).astype(BF).reshape(4, 4, 16, w)

    def along_b(j, par):
        a, b, c = axes[j]
        for d in (2, 1, 3):
            t = (b + d) % 4
            dev = device(j, a, t, c, core)
            go(remote(S[j].at[t, :, :, par], R[j].at[b, :, :, par], p2_s.at[j, par, d], p2_r.at[j, par, b], dev))
            if par == 0:
                go(remote(ST[j].at[t], RT[j].at[b], p2t_s.at[j, d], p2t_r.at[j, b], dev))

    def along_c(j, par, d, main, tail):
        a, b, c = axes[j]
        s = (b + d) % 4
        dst = canon(j, XG, (slice(None),), par, s, c, cols_of(j))
        for dc in (2, 1, 3):
            t = (c + dc) % 4
            dev = device(j, a, b, t, core)
            go(remote(main.at[s, t, :, par], dst, p3_s.at[j, par, d, dc], p3_r.at[j, par, c, s], dev))
            if par == 0:
                go(remote(tail.at[s, t], FT[j].at[c, s], p3t_s.at[j, d, dc], p3t_r.at[j, c, s], dev))
        pltpu.make_async_copy(main.at[s, c, :, par], dst, locp.at[j, par, d]).start()
        if par == 0:
            pltpu.make_async_copy(tail.at[s, c], FT[j].at[c, s], loct.at[j, d]).start()

    def pass_on(par):
        for d in (1, 3, 2):
            for j in range(3):
                s = (axes[j][1] + d) % 4
                got(R[j].at[s, :, :, par], p2_r.at[j, par, s])
                if par == 0:
                    got(RT[j].at[s], p2t_r.at[j, s])
                along_c(j, par, d, R[j], RT[j])

    def arrive(par, offsets):
        for j in range(3):
            a, b, c = axes[j]
            for db in offsets:
                s = (b + db) % 4
                f = canon(j, XG, (slice(None),), par, s, c, cols_of(j))
                landed(f, locp.at[j, par, db])
                if par == 0:
                    landed(FT[j].at[c, s], loct.at[j, db])
                for dc in (1, 2, 3):
                    t = (c + dc) % 4
                    f = canon(j, XG, (slice(None),), par, s, t, cols_of(j))
                    got(f, p3_r.at[j, par, t, s])
                    if par == 0:
                        got(FT[j].at[t, s], p3t_r.at[j, t, s])

    first, size = (0, MAIN_A + TAILS), (MAIN_A + TAILS, MAIN_A)

    def rows_of(r, par):
        main = XG[r, par].reshape(MAIN_A, D)
        return jnp.concatenate([main, XT[r]], axis=0) if par == 0 else main

    def forward(par):
        span = pl.ds(first[par], size[par])

        def hidden_tile(i, carry):
            cols = tile(i)
            rows = rows_of(0, par)
            gate_pre = jnp.dot(rows, WG[:, cols], preferred_element_type=F32)
            up_pre = jnp.dot(rows, WU[:, cols], preferred_element_type=F32)
            hidden_grad = across(rows_of(1, par), WD[cols, :])
            logistic = jax.nn.sigmoid(gate_pre)
            silu_gate = gate_pre * logistic
            HID[span, cols] = (silu_gate * up_pre).astype(BF)
            UG[span, cols] = (hidden_grad * silu_gate).astype(BF)
            GG[span, cols] = (hidden_grad * up_pre * logistic * (1.0 + gate_pre * (1.0 - logistic))).astype(BF)
            return carry

        lax.fori_loop(0, FF // 256, hidden_tile, 0)

        def slot_tile(i, carry):
            cols = tile(i)
            rows = (across(GG[span, :], WG[cols, :]) + across(UG[span, :], WU[cols, :])).astype(BF)
            SG[par, :, :, :, :, :, :, cols] = rows[:MAIN_A].reshape(2, 2, 2, 2, 2, 16, 256)
            if par == 0:
                SGT[:, cols] = rows[MAIN_A:]
            return carry

        lax.fori_loop(0, D // 256, slot_tile, 0)

    def in_tile(i, carry):
        cols = tile(i)
        parts = [XG[0, 0, :, :, :, :, :, :, cols].reshape(MAIN_A, 256), XT[0, :, cols]]
        rows = jnp.concatenate(parts + [XG[0, 1, :, :, :, :, :, :, cols].reshape(MAIN_A, 256)], axis=0)
        WG[cols, :] = over_rows(rows, GG[...]).astype(BF)
        WU[cols, :] = over_rows(rows, UG[...]).astype(BF)
        return carry

    def down_tile(i, carry):
        cols = tile(i)
        rows = jnp.concatenate([rows_of(1, 0), rows_of(1, 1)], axis=0)
        WD[cols, :] = over_rows(HID[:, cols], rows).astype(BF)
        return carry

    def back_c(par):
        for d in (2, 1, 3):
            for j in range(3):
                a, b, c = axes[j]
                t = (c + d) % 4
                dev = device(j, a, b, t, core)
                for bl in range(2):
                    if j == 0:
                        at = (par, t // 2, t % 2, slice(None), bl, slice(None))
                    elif j == 1:
                        at = (par, slice(None), bl, slice(None), (par + bl + t) % 2, t // 2)
                    else:
                        at = (par, slice(None), (par + bl + t) % 2, t // 2, t % 2, slice(None))
                    src = SG.at[at + (slice(None), cols_of(j))]
                    go(remote(src, R1[j].at[c, par, bl], r1_s.at[j, par, d, bl], r1_r.at[j, par, c, bl], dev))
        if par == 0:
            for j in range(3):
                a, b, c = axes[j]
                lo, hi = START[j], START[j] + WIDTH[j] - HALF
                rows = jnp.dot(tail_spread(j, 0), SGT[:, lo : lo + HALF], preferred_element_type=F32)
                rows = rows + jnp.dot(tail_spread(j, 1), SGT[:, hi : hi + HALF], preferred_element_type=F32)
                ST2[j][...] = rows.astype(BF).reshape(4, 4, 16, HALF)
                for d in (2, 1, 3):
                    t = (c + d) % 4
                    dev = device(j, a, b, t, core)
                    go(remote(ST2[j].at[t], RT1[j].at[c], r1t_s.at[j, d], r1t_r.at[j, c], dev))
        for j in range(3):
            c = axes[j][2]
            back_b(j, par, 0, lambda t: canon(j, SG, (), par, t, c, cols_of(j)), ST2[j].at[c])

    def back_b(j, par, d, main, tail):
        a, b, c = axes[j]
        s = (c + d) % 4
        for db in (2, 1, 3):
            t = (b + db) % 4
            dev = device(j, a, t, c, core)
            go(remote(main(t), R2[j].at[b, s, par], r2_s.at[j, par, d, db], r2_r.at[j, par, b, s], dev))
            if par == 0:
                go(remote(tail.at[t], RT2[j].at[b, s], r2t_s.at[j, d, db], r2t_r.at[j, b, s], dev))
        pltpu.make_async_copy(main(b), R2[j].at[b, s, par], l2.at[j, par, d]).start()
        if par == 0:
            pltpu.make_async_copy(tail.at[b], RT2[j].at[b, s], l2t.at[j, d]).start()

    def pass_back(par):
        for d in (1, 3, 2):
            for j in range(3):
                s = (axes[j][2] + d) % 4
                for bl in range(2):
                    got(R1[j].at[s, par, bl], r1_r.at[j, par, s, bl])
                if par == 0:
                    got(RT1[j].at[s], r1t_r.at[j, s])

                def main(t, j=j, s=s):
                    if j == 2:
                        return R1[j].at[s, par, t % 2, :, t // 2]
                    return R1[j].at[s, par, t % 2, t // 2]

                back_b(j, par, d, main, RT1[j].at[s])

    def returned(par):
        for j in range(3):
            a, b, c = axes[j]
            for dc in range(4):
                s = (c + dc) % 4
                landed(R2[j].at[b, s, par], l2.at[j, par, dc])
                if par == 0:
                    landed(RT2[j].at[b, s], l2t.at[j, dc])
                for db in (1, 2, 3):
                    t = (b + db) % 4
                    got(R2[j].at[t, s, par], r2_r.at[j, par, t, s])
                    if par == 0:
                        got(RT2[j].at[t, s], r2t_r.at[j, t, s])

    def combine(par):
        for j in range(3):
            a, b, c = axes[j]
            w = WIDTH[j]
            tails = RT2[j][...].reshape(256, HALF)
            for h in range(2):
                s = 2 * h + (par + b + c) % 2
                pick, low, high = [], [], []
                for k in range(2):
                    who = (core + k) % 2
                    at = pos[j, s, who][:, None, :]
                    row = iota((16, 16, TOK), 1)
                    hit = at * 2.0 + who.astype(F32) == row.astype(F32)
                    pick.append(jnp.where(hit, 1.0, 0.0).reshape(256, TOK))
                    hit = (at == 8.0) & (row == 2 * s + who)
                    low.append(jnp.where(hit, 1.0, 0.0).reshape(256, TOK))
                    hit = (at == 8.0) & (row == 8 + 2 * s + who)
                    high.append(jnp.where(hit, 1.0, 0.0).reshape(256, TOK))
                pick, low, high = (jnp.concatenate(p, axis=1).astype(BF) for p in (pick, low, high))
                total = over_rows(pick, R2[j][:, :, par, h].reshape(256, w))
                total = total + jnp.concatenate(
                    [over_rows(low, tails), over_rows(high, tails)[:, 2 * HALF - w :]], axis=1
                )
                i = 2 * par + h
                KEEP[j][h] = total[:TOK]
                T[j][0, i, 0] = total[TOK:].astype(BF)
                go(remote(T[j].at[0, i, 0], T[j].at[0, i, 1], ps_s.at[j, i], ps_r.at[j, i], sib))
        for j in range(3):
            a, b, c = axes[j]
            for h in range(2):
                s = 2 * h + (par + b + c) % 2
                i = 2 * par + h
                got(T[j].at[0, i, 1], ps_r.at[j, i])
                total = KEEP[j][h] + T[j][0, i, 1].astype(F32)

                @pl.when(s == a)
                def _():
                    OWN[j][...] = total

                @pl.when(s != a)
                def _():
                    T[j][1, i, 0] = total.astype(BF)
                    to_line(j, i, s).start()

    def to_line(j, i, s):
        a, b, c = axes[j]
        return remote(T[j].at[1, i, 0], T[j].at[1, a, 1], q_s.at[j, i], q_r.at[j, a], device(j, s, b, c, core))

    for j in range(3):
        a, b, c = axes[j]
        landed(metas.at[j, a, core], locm.at[j])
        for s in range(4):
            got(metas.at[j, s, 1 - core], msib_r.at[j, s])
        find_slots(j)
    for j in range(3):
        for r in range(2):
            landed(T[j].at[r, axes[j][0], core], loc.at[j, r])
            for s in range(4):
                got(T[j].at[r, s, 1 - core], sib_r.at[j, s, r])
        gather(j, 0)
        gather_tails(j)
        along_b(j, 0)
        along_c(j, 0, 0, S[j], ST[j])
    for j in range(3):
        gather(j, 1)
    for cp in early:
        cp.wait_send()
    pl.semaphore_signal(done, inc=1, device_id=sib, device_id_type=MESH)
    pass_on(0)
    arrive(0, (0,))
    for j in range(3):
        along_b(j, 1)
        along_c(j, 1, 0, S[j], ST[j])
    arrive(0, (1, 3, 2))
    for j in range(3):
        rows = FT[j][...].reshape(256, WIDTH[j])
        for r in range(2):
            XT[r, :, cols_of(j)] = jnp.dot(tail_perm(j, r), rows, preferred_element_type=F32).astype(BF)
    for i, (src, dst) in enumerate(weights):
        pltpu.make_async_copy(src.at[0], dst, wsem.at[i]).wait()
    forward(0)
    back_c(0)
    pass_on(1)
    pass_back(0)
    arrive(1, (0, 1, 3, 2))
    forward(1)
    back_c(1)
    pl.semaphore_wait(done, 1)
    returned(0)
    combine(0)
    lax.fori_loop(0, 4, in_tile, 0)
    pass_back(1)
    lax.fori_loop(4, 8, in_tile, 0)
    pltpu.make_async_copy(WG, gate_out.at[0], osem.at[0]).start()
    pltpu.make_async_copy(WU, up_out.at[0], osem.at[1]).start()
    lax.fori_loop(0, 3, down_tile, 0)
    pltpu.make_async_copy(WD, down_out.at[0], osem.at[2]).start()
    returned(1)
    combine(1)
    for j in range(3):
        a = axes[j][0]
        total = OWN[j][...]
        for d in (1, 3, 2):
            s = (a + d) % 4
            got(T[j].at[1, s, 1], q_r.at[j, s])
            total = total + T[j][1, s, 1].astype(F32)
        out[:, START[j] : START[j] + WIDTH[j]] = total.astype(BF)
    for cp in sends:
        cp.wait_send()
    for j in range(3):
        a, b, c = axes[j]
        for i in range(4):
            s = 2 * (i % 2) + (i // 2 + b + c) % 2

            @pl.when(s != a)
            def _():
                to_line(j, i, s).wait_send()

    for i, (src, dst) in enumerate(((WG, gate_out), (WU, up_out), (WD, down_out))):
        pltpu.make_async_copy(src, dst.at[0], osem.at[i]).wait()


def run(tokens, out_grad, meta, gate_weight, up_weight, down_weight):
    dma = pltpu.SemaphoreType.DMA
    vm = pltpu.VMEM
    any_spec = pl.BlockSpec(memory_space=pl.ANY)
    shape = jax.ShapeDtypeStruct
    scratch = [vm((2, 4, 2, TOK, w), BF) for w in WIDTH]
    scratch += [vm((4, 4, 2, 2, 2, 16, w), BF) for w in WIDTH]
    scratch += [vm((4, 4, 16, w), BF) for w in WIDTH] * 2
    scratch += [vm((4, 4, 16, HALF), BF)] * 3
    scratch += [vm((4, 4, 2, 2, 16, w), BF) for w in WIDTH]
    scratch += [vm((4, 4, 16, HALF), BF)] * 3
    scratch += [vm((2, TOK, w), F32) for w in WIDTH] + [vm((TOK, w), F32) for w in WIDTH]
    scratch += [vm((2, 2, 2, 2, 2, 2, 2, 16, D), BF), vm((2, TAILS, D), BF)]
    scratch += [vm((2, 2, 2, 2, 2, 2, 16, D), BF), vm((TAILS, D), BF)]
    scratch += [vm((D, FF), BF), vm((D, FF), BF), vm((FF, D), BF)] + [vm((ROWS, FF), BF)] * 3
    scratch += [vm((3, 4, 2, 16, TOK), F32)] * 2
    scratch += [dma((3, 4, 2))] * 4 + [dma((3, 4))] * 4 + [dma((3, 2)), dma((3,))]
    scratch += [dma((3, 2, 4))] * 2 + [dma((3, 4))] * 2 + [dma((3, 2, 4, 4))] * 2 + [dma((3, 4, 4))] * 2
    scratch += [dma((3, 2, 4)), dma((3, 4))]
    scratch += [dma((3, 2, 4, 2))] * 2 + [dma((3, 4))] * 2 + [dma((3, 2, 4, 4))] * 2 + [dma((3, 4, 4))] * 2
    scratch += [dma((3, 2, 4)), dma((3, 4))]
    scratch += [dma((3, 4))] * 4 + [dma((3,))] * 2 + [pltpu.SemaphoreType.REGULAR]
    outs = [shape((TOK, D), BF), shape((1, D, FF), BF), shape((1, D, FF), BF), shape((1, FF, D), BF)]
    outs += [shape((4, 4, 2, 2, 2, 16, w), BF) for w in WIDTH] + [shape((4, 4, 16, w), BF) for w in WIDTH]
    outs += [shape((4, 2, 2, 2, 2, 16, w), BF) for w in WIDTH] + [shape((4, 4, 16, HALF), BF)] * 3
    return pl.pallas_call(
        kernel,
        name="experts",
        out_shape=outs,
        in_specs=[any_spec] * 6,
        out_specs=[pl.BlockSpec(memory_space=pltpu.VMEM)] + [any_spec] * 15,
        scratch_shapes=scratch,
        compiler_params=pltpu.CompilerParams(collective_id=0, has_side_effects=True, vmem_limit_bytes=62 << 20),
    )(tokens, out_grad, meta, gate_weight, up_weight, down_weight)[:4]


def body(tokens, out_grad, expert_ids, gates, gate_weight, up_weight, down_weight):
    meta = jnp.concatenate([expert_ids.astype(F32), gates.astype(F32)], axis=1).T
    return tuple(run(tokens, out_grad, meta, gate_weight, up_weight, down_weight))


def solution(mesh):
    whole = ("node", "local")
    two, three = P(whole, None), P(whole, None, None)
    return jax.shard_map(
        body,
        mesh=mesh,
        in_specs=(two, two, two, two, three, three, three),
        out_specs=(two, three, three, three),
        check_vma=False,
    )
```

```python
import functools

import jax
import jax.numpy as jnp
from jax import lax
from jax.experimental import pallas as pl
from jax.experimental.pallas import tpu as pltpu
from jax.sharding import PartitionSpec as P

MESH = pl.DeviceIdType.MESH
BF, F32 = jnp.bfloat16, jnp.float32
D, FF, TOK, TOP, SLOTS = 2048, 768, 128, 8, 9
WIDTH = ((640, 768, 640), (640, 640, 768))
START = ((0, 640, 1408), (0, 640, 1280))
TAIL_WIDTH = (640, 768, 768)
TAIL_START = (0, 640, 1280)
HALF = 384
ROWS = 1152
MAIN_A, TAILS = 512, 128


def place():
    node, local = lax.axis_index("node"), lax.axis_index("local")
    return local // 2, (node % 8) // 2, (node // 8) * 2 + local % 2, node % 2


def order(j, x, y, z):
    return ((x, y, z), (y, z, x), (z, x, y))[j]


def device(j, a, b, c, core):
    x, y, z = ((a, b, c), (c, a, b), (b, c, a))[j]
    return ((z // 2) * 8 + y * 2 + core, x * 2 + z % 2)


def canon(j, ref, lead, par, b, c, cols):
    q = (par + b + c) % 2
    every = slice(None)
    if j == 0:
        at = (par, c // 2, c % 2, b // 2, b % 2, every)
    elif j == 1:
        at = (par, b // 2, b % 2, every, q, c // 2)
    else:
        at = (par, every, q, c // 2, c % 2, b // 2)
    return ref.at[lead + at + (every, cols)]


def remote(src, dst, ssem, rsem, dev):
    return pltpu.make_async_remote_copy(
        src_ref=src, dst_ref=dst, send_sem=ssem, recv_sem=rsem, device_id=dev, device_id_type=MESH
    )


def greet(partners):
    barrier = pltpu.get_barrier_semaphore()
    for dev in partners:
        pl.semaphore_signal(barrier, inc=1, device_id=dev, device_id_type=MESH)
    pl.semaphore_wait(barrier, len(partners))


def partners_of(x, y, z, core):
    out = [device(0, x, y, z, 1 - core)]
    for d in (1, 2, 3):
        out.append(device(0, (x + d) % 4, y, z, core))
        out.append(device(0, x, (y + d) % 4, z, core))
        out.append(device(0, x, y, (z + d) % 4, core))
    return out


def iota(shape, dim):
    return lax.broadcasted_iota(jnp.int32, shape, dim)


def tail_perm(j, array):
    row, col = iota((128, 256), 0), iota((128, 256), 1)
    core, x, y, z = row % 2, (row // 2) % 4, (row // 8) % 4, row // 32
    a, b, c = order(j, x, y, z)
    want = c * 64 + b * 16 + array * 8 + a * 2 + core
    return (col == want).astype(F32).astype(BF)


def tail_spread(j, half):
    row, col = iota((256, 128), 0), iota((256, 128), 1)
    c, b, h, a, core = row // 64, (row // 16) % 4, (row // 8) % 2, (row // 2) % 4, row % 2
    x, y, z = ((a, b, c), (c, a, b), (b, c, a))[j]
    return ((col == z * 32 + y * 8 + x * 2 + core) & (h == half)).astype(F32).astype(BF)


def over_rows(left, right):
    return lax.dot_general(left, right, (((0,), (0,)), ((), ())), preferred_element_type=F32)


def across(left, right):
    return lax.dot_general(left, right, (((1,), (1,)), ((), ())), preferred_element_type=F32)


def tile(i):
    return pl.ds(pl.multiple_of(i * 256, 256), 256)


def by_two(refs):
    return tuple(refs[2 * j : 2 * j + 2] for j in range(3))


def kernel(tok, grad, ids, gates, gate_w, up_w, down_w, out, gate_out, up_out, down_out, *rest):
    R, R1, RT, RT1, scr = by_two(rest[:6]), by_two(rest[6:12]), rest[12:15], rest[15:18], rest[18:]
    T, S, R2 = (by_two(scr[6 * i : 6 * i + 6]) for i in range(3))
    ST, FT, ST2, RT2, KEEP = (scr[18 + 3 * i : 21 + 3 * i] for i in range(5))
    PK, OWN, XG, XT, SG, SGT, WG, WU, WD, HID, GG, UG, meta, metas, pos = scr[33:48]
    (ag_s, ag_r, sib_s, sib_r, mag_s, mag_r, msib_s, msib_r, loc, locm,
     p2_s, p2_r, p2t_s, p2t_r, p3_s, p3_r, p3t_s, p3t_r, locp, loct,
     r1_s, r1_r, r1t_s, r1t_r, r2_s, r2_r, r2t_s, r2t_r, l2, l2t,
     ps_s, ps_r, q_s, q_r, wsem, osem, done) = scr[48:]
    x, y, z, core = place()
    axes = [order(j, x, y, z) for j in range(3)]
    sib = device(0, x, y, z, 1 - core)
    weights = ((gate_w, WG), (up_w, WU), (down_w, WD))
    for i, (src, dst) in enumerate(weights):
        pltpu.make_async_copy(src.at[0], dst, wsem.at[i]).start()
    meta[:TOP] = ids[...].astype(F32)
    meta[TOP:] = gates[...].astype(F32)
    greet(partners_of(x, y, z, core))
    ins = (tok, grad)
    sends, early = [], []

    def go(cp, kept=sends):
        cp.start()
        kept.append(cp)

    def got(ref, rsem):
        remote(ref, ref, ag_s.at[0, 0, 0], rsem, sib).wait_recv()

    def landed(ref, sem):
        pltpu.make_async_copy(ref, ref, sem).wait()

    def cols_of(i, j):
        return pl.ds(START[i][j], WIDTH[i][j])

    for j in range(3):
        a, b, c = axes[j]
        for d in (2, 1, 3):
            dev = device(j, (a + d) % 4, b, c, core)
            go(remote(meta, metas.at[j, a, core], mag_s.at[j, d], mag_r.at[j, a], dev))
    for d in (2, 1, 3):
        for j in range(3):
            a, b, c = axes[j]
            dev = device(j, (a + d) % 4, b, c, core)
            for r in range(2):
                src = ins[r].at[:, cols_of(r, j)]
                go(remote(src, T[j][r].at[a, core], ag_s.at[j, d, r], ag_r.at[j, a, r], dev))
    for j in range(3):
        a, b, c = axes[j]
        go(remote(meta, metas.at[j, a, core], msib_s.at[j, a], msib_r.at[j, a], sib))
        pltpu.make_async_copy(meta, metas.at[j, a, core], locm.at[j]).start()
        for r in range(2):
            src = ins[r].at[:, cols_of(r, j)]
            go(remote(src, T[j][r].at[a, core], sib_s.at[j, a, r], sib_r.at[j, a, r], sib))
            pltpu.make_async_copy(src, T[j][r].at[a, core], loc.at[j, r]).start()

    for d in (1, 3, 2):
        for j in range(3):
            s = (axes[j][0] + d) % 4
            m = metas.at[j, s, core]
            got(m, mag_r.at[j, s])
            go(remote(m, m, msib_s.at[j, s], msib_r.at[j, s], sib))
        for j in range(3):
            s = (axes[j][0] + d) % 4
            for r in range(2):
                t = T[j][r].at[s, core]
                got(t, ag_r.at[j, s, r])
                go(remote(t, t, sib_s.at[j, s, r], sib_r.at[j, s, r], sib), early)

    before = (iota((TOK, TOK), 0) < iota((TOK, TOK), 1)).astype(F32).astype(BF)

    def one_hot(j, s, gate, last):
        a = axes[j][0]
        e = iota((16, 1), 0)
        dev = device(j, a, e // 4, e % 4, core)
        expert = (dev[0] * 8 + dev[1]).astype(F32)
        parts = []
        for k in range(2):
            info = metas[j, s, k]
            value = jnp.ones((16, TOK), F32)
            if gate:
                value = jnp.zeros((16, TOK), F32)
                for i in range(TOP):
                    hit = info[i : i + 1, :] == expert
                    value = value + jnp.where(hit, info[TOP + i : TOP + i + 1, :], 0.0)
            at = pos[j, s, k][:, None, :]
            if last:
                hit = (at == 8.0) & (iota((16, 8, TOK), 1) == 2 * s + k)
            else:
                hit = at * 2.0 + k == iota((16, 16, TOK), 1).astype(F32)
            parts.append(jnp.where(hit, value[:, None, :], 0.0).reshape(128 if last else 256, TOK))
        return jnp.concatenate(parts, axis=1).astype(BF)

    def find_slots(j):
        a = axes[j][0]
        e = iota((16, 1), 0)
        dev = device(j, a, e // 4, e % 4, core)
        expert = (dev[0] * 8 + dev[1]).astype(F32)
        for s in range(4):
            for k in range(2):
                info = metas[j, s, k]
                named = jnp.zeros((16, TOK), F32)
                for i in range(TOP):
                    named = named + jnp.where(info[i : i + 1, :] == expert, 1.0, 0.0)
                earlier = jnp.dot(named.astype(BF), before, preferred_element_type=F32)
                pos[j, s, k] = jnp.where(named > 0.5, earlier, -1.0)

    def gather(j, par):
        a, b, c = axes[j]
        for h in range(2):
            s = 2 * h + (par + b + c) % 2
            for r in range(2):
                w = WIDTH[r][j]
                rows = T[j][r][s].reshape(2 * TOK, w)
                main = jnp.dot(one_hot(j, s, r == 1, False), rows, preferred_element_type=F32)
                S[j][r][:, :, par, h] = main.astype(BF).reshape(4, 4, 16, w)

    def gather_tails(j):
        tails = []
        for r in range(2):
            w = WIDTH[r][j]
            rows = jnp.zeros((TAILS, w), F32)
            for s in range(4):
                picked = T[j][r][s].reshape(2 * TOK, w)
                rows = rows + jnp.dot(one_hot(j, s, r == 1, True), picked, preferred_element_type=F32)
            left = START[r][j] - TAIL_START[j]
            right = TAIL_WIDTH[j] - w - left
            rows = [rows]
            if left:
                rows = [jnp.zeros((TAILS, left), F32)] + rows
            if right:
                rows = rows + [jnp.zeros((TAILS, right), F32)]
            tails.append(jnp.concatenate(rows, axis=1).reshape(16, 8, TAIL_WIDTH[j]))
        ST[j][...] = jnp.concatenate(tails, axis=1).astype(BF).reshape(4, 4, 16, TAIL_WIDTH[j])

    def along_b(j, par):
        a, b, c = axes[j]
        for d in (2, 1, 3):
            t = (b + d) % 4
            dev = device(j, a, t, c, core)
            for r in range(2):
                src, dst = S[j][r].at[t, :, par], R[j][r].at[b, :, par]
                go(remote(src, dst, p2_s.at[j, par, d, r], p2_r.at[j, par, b, r], dev))

    def along_c(j, par, d, main):
        a, b, c = axes[j]
        s = (b + d) % 4
        for r in range(2):
            dst = canon(j, XG, (r,), par, s, c, cols_of(r, j))
            for dc in (2, 1, 3):
                t = (c + dc) % 4
                dev = device(j, a, b, t, core)
                go(remote(main[r].at[s, t, par], dst, p3_s.at[j, par, d, dc, r], p3_r.at[j, par, c, s, r], dev))
            pltpu.make_async_copy(main[r].at[s, c, par], dst, locp.at[j, par, d, r]).start()

    def tails_along_b(j):
        a, b, c = axes[j]
        for d in (2, 1, 3):
            t = (b + d) % 4
            dev = device(j, a, t, c, core)
            go(remote(ST[j].at[t], RT[j].at[b], p2t_s.at[j, d], p2t_r.at[j, b], dev))

    def tails_along_c(j, d, tail):
        a, b, c = axes[j]
        s = (b + d) % 4
        for dc in (2, 1, 3):
            t = (c + dc) % 4
            dev = device(j, a, b, t, core)
            go(remote(tail.at[s, t], FT[j].at[c, s], p3t_s.at[j, d, dc], p3t_r.at[j, c, s], dev))
        pltpu.make_async_copy(tail.at[s, c], FT[j].at[c, s], loct.at[j, d]).start()

    def pass_on(par):
        for d in (1, 3, 2):
            for j in range(3):
                s = (axes[j][1] + d) % 4
                for r in range(2):
                    got(R[j][r].at[s, :, par], p2_r.at[j, par, s, r])
                along_c(j, par, d, R[j])

    def pass_tails():
        for d in (1, 3, 2):
            for j in range(3):
                s = (axes[j][1] + d) % 4
                got(RT[j].at[s], p2t_r.at[j, s])
                tails_along_c(j, d, RT[j])

    def arrive(par, offsets):
        for j in range(3):
            a, b, c = axes[j]
            for db in offsets:
                s = (b + db) % 4
                for r in range(2):
                    landed(canon(j, XG, (r,), par, s, c, cols_of(r, j)), locp.at[j, par, db, r])
                    for dc in (1, 2, 3):
                        t = (c + dc) % 4
                        got(canon(j, XG, (r,), par, s, t, cols_of(r, j)), p3_r.at[j, par, t, s, r])

    def arrive_tails():
        for j in range(3):
            a, b, c = axes[j]
            for db in range(4):
                s = (b + db) % 4
                landed(FT[j].at[c, s], loct.at[j, db])
                for dc in (1, 2, 3):
                    t = (c + dc) % 4
                    got(FT[j].at[t, s], p3t_r.at[j, t, s])
            rows = FT[j][...].reshape(256, TAIL_WIDTH[j])
            for r in range(2):
                picked = jnp.dot(tail_perm(j, r), rows, preferred_element_type=F32).astype(BF)
                left = START[r][j] - TAIL_START[j]
                XT[r, :, cols_of(r, j)] = picked[:, left : left + WIDTH[r][j]]

    first, size = (0, MAIN_A + TAILS), (MAIN_A + TAILS, MAIN_A)

    def rows_of(r, par):
        main = XG[r, par].reshape(MAIN_A, D)
        return jnp.concatenate([main, XT[r]], axis=0) if par == 0 else main

    def forward(par):
        span = pl.ds(first[par], size[par])

        def hidden_tile(i, carry):
            cols = tile(i)
            rows = rows_of(0, par)
            gate_pre = jnp.dot(rows, WG[:, cols], preferred_element_type=F32)
            up_pre = jnp.dot(rows, WU[:, cols], preferred_element_type=F32)
            hidden_grad = across(rows_of(1, par), WD[cols, :])
            logistic = jax.nn.sigmoid(gate_pre)
            silu_gate = gate_pre * logistic
            HID[span, cols] = (silu_gate * up_pre).astype(BF)
            UG[span, cols] = (hidden_grad * silu_gate).astype(BF)
            GG[span, cols] = (hidden_grad * up_pre * logistic * (1.0 + gate_pre * (1.0 - logistic))).astype(BF)
            return carry

        lax.fori_loop(0, FF // 256, hidden_tile, 0)

        def slot_tile(i, carry):
            cols = tile(i)
            rows = (across(GG[span, :], WG[cols, :]) + across(UG[span, :], WU[cols, :])).astype(BF)
            SG[par, :, :, :, :, :, :, cols] = rows[:MAIN_A].reshape(2, 2, 2, 2, 2, 16, 256)
            if par == 0:
                SGT[:, cols] = rows[MAIN_A:]
            return carry

        ready = 0
        for j in range(3):
            stop = -(-(START[par][j] + WIDTH[par][j]) // 256)
            lax.fori_loop(ready, stop, slot_tile, 0)
            ready = stop
            back_c(par, j)

    def in_tile(i, carry):
        cols = tile(i)
        parts = [XG[0, 0, :, :, :, :, :, :, cols].reshape(MAIN_A, 256), XT[0, :, cols]]
        rows = jnp.concatenate(parts + [XG[0, 1, :, :, :, :, :, :, cols].reshape(MAIN_A, 256)], axis=0)
        WG[cols, :] = over_rows(rows, GG[...]).astype(BF)
        WU[cols, :] = over_rows(rows, UG[...]).astype(BF)
        return carry

    def down_tile(i, carry):
        cols = tile(i)
        rows = jnp.concatenate([rows_of(1, 0), rows_of(1, 1)], axis=0)
        WD[cols, :] = over_rows(HID[:, cols], rows).astype(BF)
        return carry

    def back_c(par, j):
        a, b, c = axes[j]
        for d in (2, 1, 3):
            t = (c + d) % 4
            dev = device(j, a, b, t, core)
            for bl in range(2):
                if j == 0:
                    at = (par, t // 2, t % 2, slice(None), bl, slice(None))
                elif j == 1:
                    at = (par, slice(None), bl, slice(None), (par + bl + t) % 2, t // 2)
                else:
                    at = (par, slice(None), (par + bl + t) % 2, t // 2, t % 2, slice(None))
                src = SG.at[at + (slice(None), cols_of(par, j))]
                go(remote(src, R1[j][par].at[c, bl], r1_s.at[j, par, d, bl], r1_r.at[j, par, c, bl], dev))
        if par == 0:
            lo, hi = TAIL_START[j], TAIL_START[j] + TAIL_WIDTH[j] - HALF
            rows = jnp.dot(tail_spread(j, 0), SGT[:, lo : lo + HALF], preferred_element_type=F32)
            rows = rows + jnp.dot(tail_spread(j, 1), SGT[:, hi : hi + HALF], preferred_element_type=F32)
            ST2[j][...] = rows.astype(BF).reshape(4, 4, 16, HALF)
            for d in (2, 1, 3):
                t = (c + d) % 4
                dev = device(j, a, b, t, core)
                go(remote(ST2[j].at[t], RT1[j].at[c], r1t_s.at[j, d], r1t_r.at[j, c], dev))
        back_b(j, par, 0, lambda t: canon(j, SG, (), par, t, c, cols_of(par, j)), ST2[j].at[c])

    def back_b(j, par, d, main, tail):
        a, b, c = axes[j]
        s = (c + d) % 4
        for db in (2, 1, 3):
            t = (b + db) % 4
            dev = device(j, a, t, c, core)
            go(remote(main(t), R2[j][par].at[b, s], r2_s.at[j, par, d, db], r2_r.at[j, par, b, s], dev))
            if par == 0:
                go(remote(tail.at[t], RT2[j].at[b, s], r2t_s.at[j, d, db], r2t_r.at[j, b, s], dev))
        pltpu.make_async_copy(main(b), R2[j][par].at[b, s], l2.at[j, par, d]).start()
        if par == 0:
            pltpu.make_async_copy(tail.at[b], RT2[j].at[b, s], l2t.at[j, d]).start()

    def pass_back(par):
        for d in (1, 3, 2):
            for j in range(3):
                s = (axes[j][2] + d) % 4
                for bl in range(2):
                    got(R1[j][par].at[s, bl], r1_r.at[j, par, s, bl])
                if par == 0:
                    got(RT1[j].at[s], r1t_r.at[j, s])

                def main(t, j=j, s=s):
                    if j == 2:
                        return R1[j][par].at[s, t % 2, :, t // 2]
                    return R1[j][par].at[s, t % 2, t // 2]

                back_b(j, par, d, main, RT1[j].at[s])

    def returned(par, j):
        a, b, c = axes[j]
        for dc in (0, 1, 3, 2):
            s = (c + dc) % 4
            landed(R2[j][par].at[b, s], l2.at[j, par, dc])
            for db in (1, 2, 3):
                t = (b + db) % 4
                got(R2[j][par].at[t, s], r2_r.at[j, par, t, s])

    def tails_returned(j):
        a, b, c = axes[j]
        for dc in (0, 1, 3, 2):
            s = (c + dc) % 4
            landed(RT2[j].at[b, s], l2t.at[j, dc])
            for db in (1, 2, 3):
                t = (b + db) % 4
                got(RT2[j].at[t, s], r2t_r.at[j, t, s])

    def prepare(par, j):
        a, b, c = axes[j]
        left, w = START[par][j] - TAIL_START[j], WIDTH[par][j]
        tails = RT2[j][...].reshape(256, HALF)
        for h in range(2):
            s = 2 * h + (par + b + c) % 2
            pick, low, high = [], [], []
            for k in range(2):
                who = (core + k) % 2
                at = pos[j, s, who][:, None, :]
                row = iota((16, 16, TOK), 1)
                hit = at * 2.0 + who.astype(F32) == row.astype(F32)
                pick.append(jnp.where(hit, 1.0, 0.0).reshape(256, TOK))
                hit = (at == 8.0) & (row == 2 * s + who)
                low.append(jnp.where(hit, 1.0, 0.0).reshape(256, TOK))
                hit = (at == 8.0) & (row == 8 + 2 * s + who)
                high.append(jnp.where(hit, 1.0, 0.0).reshape(256, TOK))
            pick, low, high = (jnp.concatenate(p, axis=1).astype(BF) for p in (pick, low, high))
            PK[j, h] = pick
            both = [over_rows(low, tails), over_rows(high, tails)[:, 2 * HALF - TAIL_WIDTH[j] :]]
            KEEP[j][h, :, :w] = jnp.concatenate(both, axis=1)[:, left : left + w]

    def combine(par):
        swaps = []
        for j in range(3):
            returned(par, j)
            w = WIDTH[par][j]
            for h in range(2):
                total = KEEP[j][h, :, :w] + over_rows(PK[j, h], R2[j][par][:, :, h].reshape(256, w))
                KEEP[j][h, :TOK, :w] = total[:TOK]
                T[j][par][h, 0] = total[TOK:].astype(BF)
                mine, theirs = T[j][par].at[h, 0], T[j][par].at[h, 1]
                cp = remote(mine, theirs, ps_s.at[j, 2 * par + h], ps_r.at[j, 2 * par + h], sib)
                cp.start()
                swaps.append(cp)
        for j in range(3):
            a, b, c = axes[j]
            w = WIDTH[par][j]
            for h in range(2):
                s = 2 * h + (par + b + c) % 2
                swaps[2 * j + h].wait_send()
                got(T[j][par].at[h, 1], ps_r.at[j, 2 * par + h])
                total = KEEP[j][h, :TOK, :w] + T[j][par][h, 1].astype(F32)

                @pl.when(s == a)
                def _():
                    OWN[:, cols_of(par, j)] = total

                @pl.when(s != a)
                def _():
                    T[j][par][h, 0] = total.astype(BF)
                    to_line(j, par, h, s).start()

    def to_line(j, par, h, s):
        a, b, c = axes[j]
        dst = T[j][par].at[2 + a // 2, a % 2]
        return remote(T[j][par].at[h, 0], dst, q_s.at[j, 2 * par + h], q_r.at[j, a], device(j, s, b, c, core))

    for j in range(3):
        a, b, c = axes[j]
        landed(metas.at[j, a, core], locm.at[j])
        for s in range(4):
            got(metas.at[j, s, 1 - core], msib_r.at[j, s])
        find_slots(j)
    for j in range(3):
        for r in range(2):
            landed(T[j][r].at[axes[j][0], core], loc.at[j, r])
            for s in range(4):
                got(T[j][r].at[s, 1 - core], sib_r.at[j, s, r])
        gather(j, 0)
        along_b(j, 0)
        along_c(j, 0, 0, S[j])
    for j in range(3):
        gather_tails(j)
        tails_along_b(j)
        tails_along_c(j, 0, ST[j])
    for j in range(3):
        gather(j, 1)
    for cp in early:
        cp.wait_send()
    pl.semaphore_signal(done, inc=1, device_id=sib, device_id_type=MESH)
    pass_on(0)
    pass_tails()
    for j in range(3):
        along_b(j, 1)
        along_c(j, 1, 0, S[j])
    arrive(0, (0, 1, 3, 2))
    arrive_tails()
    for i, (src, dst) in enumerate(weights):
        pltpu.make_async_copy(src.at[0], dst, wsem.at[i]).wait()
    forward(0)
    pass_on(1)
    pass_back(0)
    arrive(1, (0, 1, 3, 2))
    forward(1)
    pl.semaphore_wait(done, 1)
    for j in range(3):
        tails_returned(j)
        prepare(0, j)
    combine(0)
    for j in range(3):
        prepare(1, j)
    pass_back(1)
    lax.fori_loop(0, 8, in_tile, 0)
    pltpu.make_async_copy(WG, gate_out.at[0], osem.at[0]).start()
    pltpu.make_async_copy(WU, up_out.at[0], osem.at[1]).start()
    lax.fori_loop(0, 3, down_tile, 0)
    pltpu.make_async_copy(WD, down_out.at[0], osem.at[2]).start()
    combine(1)
    for m in range(2):

        @pl.when((x + y + z) % 2 == m)
        def _():
            for j in range(3):
                a = axes[j][0]
                total = OWN[:, cols_of(m, j)]
                for d in (1, 3, 2):
                    s = (a + d) % 4
                    part = T[j][m].at[2 + s // 2, s % 2]
                    got(part, q_r.at[j, s])
                    total = total + part[...].astype(F32)
                out[:, cols_of(m, j)] = total.astype(BF)

    for cp in sends:
        cp.wait_send()
    for j in range(3):
        a, b, c = axes[j]
        for i in range(4):
            s = 2 * (i % 2) + (i // 2 + b + c) % 2

            @pl.when(s != a)
            def _():
                to_line(j, i // 2, i % 2, s).wait_send()

    for i, (src, dst) in enumerate(((WG, gate_out), (WU, up_out), (WD, down_out))):
        pltpu.make_async_copy(src, dst.at[0], osem.at[i]).wait()


def run(tokens, out_grad, ids, gates, gate_weight, up_weight, down_weight):
    dma = pltpu.SemaphoreType.DMA
    vm = pltpu.VMEM
    any_spec = pl.BlockSpec(memory_space=pl.ANY)
    vm_spec = pl.BlockSpec(memory_space=pltpu.VMEM)
    shape = jax.ShapeDtypeStruct
    both = [WIDTH[i][j] for j in range(3) for i in range(2)]
    scratch = [vm((4, 2, TOK, w), BF) for w in both]
    scratch += [vm((4, 4, 2, 2, 16, w), BF) for w in both]
    scratch += [vm((4, 4, 2, 16, w), BF) for w in both]
    scratch += [vm((4, 4, 16, w), BF) for w in TAIL_WIDTH] * 2
    scratch += [vm((4, 4, 16, HALF), BF)] * 6
    scratch += [vm((2, 2 * TOK, 768), F32)] * 3
    scratch += [vm((3, 2, 256, 256), BF), vm((TOK, D), F32)]
    scratch += [vm((2, 2, 2, 2, 2, 2, 2, 16, D), BF), vm((2, TAILS, D), BF)]
    scratch += [vm((2, 2, 2, 2, 2, 2, 16, D), BF), vm((TAILS, D), BF)]
    scratch += [vm((D, FF), BF), vm((D, FF), BF), vm((FF, D), BF)] + [vm((ROWS, FF), BF)] * 3
    scratch += [vm((2 * TOP, TOK), F32)] + [vm((3, 4, 2, 16, TOK), F32)] * 2
    scratch += [dma((3, 4, 2))] * 4 + [dma((3, 4))] * 4 + [dma((3, 2)), dma((3,))]
    scratch += [dma((3, 2, 4, 2))] * 2 + [dma((3, 4))] * 2 + [dma((3, 2, 4, 4, 2))] * 2 + [dma((3, 4, 4))] * 2
    scratch += [dma((3, 2, 4, 2)), dma((3, 4))]
    scratch += [dma((3, 2, 4, 2))] * 2 + [dma((3, 4))] * 2 + [dma((3, 2, 4, 4))] * 2 + [dma((3, 4, 4))] * 2
    scratch += [dma((3, 2, 4)), dma((3, 4))]
    scratch += [dma((3, 4))] * 4 + [dma((3,))] * 2 + [pltpu.SemaphoreType.REGULAR]
    outs = [shape((TOK, D), BF), shape((1, D, FF), BF), shape((1, D, FF), BF), shape((1, FF, D), BF)]
    outs += [shape((4, 4, 2, 2, 16, w), BF) for w in both]
    outs += [shape((4, 2, 2, 2, 16, w), BF) for w in both]
    outs += [shape((4, 4, 16, w), BF) for w in TAIL_WIDTH] + [shape((4, 4, 16, HALF), BF)] * 3
    return pl.pallas_call(
        kernel,
        name="experts",
        out_shape=outs,
        in_specs=[any_spec] * 2 + [vm_spec] * 2 + [any_spec] * 3,
        out_specs=[vm_spec] + [any_spec] * 21,
        scratch_shapes=scratch,
        compiler_params=pltpu.CompilerParams(collective_id=0, has_side_effects=True, vmem_limit_bytes=62 << 20),
    )(tokens, out_grad, ids, gates, gate_weight, up_weight, down_weight)[:4]


def body(tokens, out_grad, expert_ids, gates, gate_weight, up_weight, down_weight):
    return tuple(run(tokens, out_grad, expert_ids.T, gates.T, gate_weight, up_weight, down_weight))


def solution(mesh):
    whole = ("node", "local")
    two, three = P(whole, None), P(whole, None, None)
    return jax.shard_map(
        body,
        mesh=mesh,
        in_specs=(two, two, two, two, three, three, three),
        out_specs=(two, three, three, three),
        check_vma=False,
    )
```

```python
import functools

import jax
import jax.numpy as jnp
from jax import lax
from jax.experimental import pallas as pl
from jax.experimental.pallas import tpu as pltpu
from jax.sharding import PartitionSpec as P

MESH = pl.DeviceIdType.MESH
BF, F32 = jnp.bfloat16, jnp.float32
D, FF, TOK, TOP, SLOTS = 2048, 768, 128, 8, 9
WIDTH = ((640, 768, 640), (640, 640, 768))
START = ((0, 640, 1408), (0, 640, 1280))
TAIL_WIDTH = (640, 768, 768)
TAIL_START = (0, 640, 1280)
HALF = 384
ROWS = 1152
MAIN_A, TAILS = 512, 128


def place():
    node, local = lax.axis_index("node"), lax.axis_index("local")
    return local // 2, (node % 8) // 2, (node // 8) * 2 + local % 2, node % 2


def order(j, x, y, z):
    return ((x, y, z), (y, z, x), (z, x, y))[j]


def device(j, a, b, c, core):
    x, y, z = ((a, b, c), (c, a, b), (b, c, a))[j]
    return ((z // 2) * 8 + y * 2 + core, x * 2 + z % 2)


def canon(j, ref, lead, par, b, c, cols):
    q = (par + b + c) % 2
    every = slice(None)
    if j == 0:
        at = (par, c // 2, c % 2, b // 2, b % 2, every)
    elif j == 1:
        at = (par, b // 2, b % 2, every, q, c // 2)
    else:
        at = (par, every, q, c // 2, c % 2, b // 2)
    return ref.at[lead + at + (every, cols)]


def remote(src, dst, ssem, rsem, dev):
    return pltpu.make_async_remote_copy(
        src_ref=src, dst_ref=dst, send_sem=ssem, recv_sem=rsem, device_id=dev, device_id_type=MESH
    )


def greet(partners):
    barrier = pltpu.get_barrier_semaphore()
    for dev in partners:
        pl.semaphore_signal(barrier, inc=1, device_id=dev, device_id_type=MESH)
    pl.semaphore_wait(barrier, len(partners))


def partners_of(x, y, z, core):
    out = [device(0, x, y, z, 1 - core)]
    for d in (1, 2, 3):
        out.append(device(0, (x + d) % 4, y, z, core))
        out.append(device(0, x, (y + d) % 4, z, core))
        out.append(device(0, x, y, (z + d) % 4, core))
    return out


def iota(shape, dim):
    return lax.broadcasted_iota(jnp.int32, shape, dim)


def tail_perm(j, array):
    row, col = iota((128, 256), 0), iota((128, 256), 1)
    core, x, y, z = row % 2, (row // 2) % 4, (row // 8) % 4, row // 32
    a, b, c = order(j, x, y, z)
    want = c * 64 + b * 16 + array * 8 + a * 2 + core
    return (col == want).astype(F32).astype(BF)


def tail_spread(j, half):
    row, col = iota((256, 128), 0), iota((256, 128), 1)
    c, b, h, a, core = row // 64, (row // 16) % 4, (row // 8) % 2, (row // 2) % 4, row % 2
    x, y, z = ((a, b, c), (c, a, b), (b, c, a))[j]
    return ((col == z * 32 + y * 8 + x * 2 + core) & (h == half)).astype(F32).astype(BF)


def over_rows(left, right):
    return lax.dot_general(left, right, (((0,), (0,)), ((), ())), preferred_element_type=F32)


def across(left, right):
    return lax.dot_general(left, right, (((1,), (1,)), ((), ())), preferred_element_type=F32)


def tile(i):
    return pl.ds(pl.multiple_of(i * 256, 256), 256)


def by_two(refs):
    return tuple(refs[2 * j : 2 * j + 2] for j in range(3))


def kernel(tok, grad, ids, gates, gate_w, up_w, down_w, out, gate_out, up_out, down_out, *rest):
    R, R1, RT, RT1, scr = by_two(rest[:6]), by_two(rest[6:12]), rest[12:15], rest[15:18], rest[18:]
    T, S, R2 = (by_two(scr[6 * i : 6 * i + 6]) for i in range(3))
    ST, FT, ST2, RT2, KEEP = (scr[18 + 3 * i : 21 + 3 * i] for i in range(5))
    PK, OWN, XG, XT, SG, SGT, HID, GG, UG, meta, metas, pos = scr[33:45]
    (ag_s, ag_r, sib_s, sib_r, mag_s, mag_r, msib_s, msib_r, loc, locm,
     p2_s, p2_r, p2t_s, p2t_r, p3_s, p3_r, p3t_s, p3t_r, locp, loct,
     r1_s, r1_r, r1t_s, r1t_r, r2_s, r2_r, r2t_s, r2t_r, l2, l2t,
     ps_s, ps_r, q_s, q_r, wsem, done) = scr[45:]
    WG, WU, WD = gate_out.at[0], up_out.at[0], down_out.at[0]
    x, y, z, core = place()
    axes = [order(j, x, y, z) for j in range(3)]
    sib = device(0, x, y, z, 1 - core)
    weights = ((gate_w, WG), (up_w, WU), (down_w, WD))
    for i, (src, dst) in enumerate(weights):
        pltpu.make_async_copy(src.at[0], dst, wsem.at[i]).start()
    meta[:TOP] = ids[...].astype(F32)
    meta[TOP:] = gates[...].astype(F32)
    greet(partners_of(x, y, z, core))
    ins = (tok, grad)
    sends, early = [], []

    def go(cp, kept=sends):
        cp.start()
        kept.append(cp)

    def got(ref, rsem):
        remote(ref, ref, ag_s.at[0, 0, 0], rsem, sib).wait_recv()

    def landed(ref, sem):
        pltpu.make_async_copy(ref, ref, sem).wait()

    def cols_of(i, j):
        return pl.ds(START[i][j], WIDTH[i][j])

    for j in range(3):
        a, b, c = axes[j]
        for d in (2, 1, 3):
            dev = device(j, (a + d) % 4, b, c, core)
            go(remote(meta, metas.at[j, a, core], mag_s.at[j, d], mag_r.at[j, a], dev))
    def to_lines(r):
        for d in (1, 3):
            for j in range(3):
                a, b, c = axes[j]
                dev = device(j, (a + d) % 4, b, c, core)
                src = ins[r].at[:, cols_of(r, j)]
                go(remote(src, T[j][r].at[a, core], ag_s.at[j, d, r], ag_r.at[j, a, r], dev))

    def metas_across(d):
        for j in range(3):
            s = (axes[j][0] + d) % 4
            m = metas.at[j, s, core]
            got(m, mag_r.at[j, s])
            go(remote(m, m, msib_s.at[j, s], msib_r.at[j, s], sib))

    def rows_across(d, r):
        for j in range(3):
            s = (axes[j][0] + d) % 4
            t = T[j][r].at[s, core]
            got(t, ag_r.at[j, s, r])
            go(remote(t, t, sib_s.at[j, s, r], sib_r.at[j, s, r], sib), early)

    def second_hop(r):
        for j in range(3):
            a, b, c = axes[j]
            way = 1 - 2 * core
            t = T[j][r].at[(a - way) % 4, core]
            dev = device(j, (a + way) % 4, b, c, core)
            go(remote(t, t, ag_s.at[j, 2, r], ag_r.at[j, (a - way) % 4, r], dev), early)

    to_lines(0)
    for j in range(3):
        a, b, c = axes[j]
        go(remote(meta, metas.at[j, a, core], msib_s.at[j, a], msib_r.at[j, a], sib))
        pltpu.make_async_copy(meta, metas.at[j, a, core], locm.at[j]).start()
        for r in range(2):
            src = ins[r].at[:, cols_of(r, j)]
            go(remote(src, T[j][r].at[a, core], sib_s.at[j, a, r], sib_r.at[j, a, r], sib))
            pltpu.make_async_copy(src, T[j][r].at[a, core], loc.at[j, r]).start()
    for d in (1, 3):
        metas_across(d)
        rows_across(d, 0)
    second_hop(0)
    to_lines(1)
    metas_across(2)
    rows_across(2, 0)

    before = (iota((TOK, TOK), 0) < iota((TOK, TOK), 1)).astype(F32).astype(BF)

    def one_hot(j, s, gate, last):
        a = axes[j][0]
        e = iota((16, 1), 0)
        dev = device(j, a, e // 4, e % 4, core)
        expert = (dev[0] * 8 + dev[1]).astype(F32)
        parts = []
        for k in range(2):
            info = metas[j, s, k]
            value = jnp.ones((16, TOK), F32)
            if gate:
                value = jnp.zeros((16, TOK), F32)
                for i in range(TOP):
                    hit = info[i : i + 1, :] == expert
                    value = value + jnp.where(hit, info[TOP + i : TOP + i + 1, :], 0.0)
            at = pos[j, s, k][:, None, :]
            if last:
                hit = (at == 8.0) & (iota((16, 8, TOK), 1) == 2 * s + k)
            else:
                hit = at * 2.0 + k == iota((16, 16, TOK), 1).astype(F32)
            parts.append(jnp.where(hit, value[:, None, :], 0.0).reshape(128 if last else 256, TOK))
        return jnp.concatenate(parts, axis=1).astype(BF)

    def find_slots(j):
        a = axes[j][0]
        e = iota((16, 1), 0)
        dev = device(j, a, e // 4, e % 4, core)
        expert = (dev[0] * 8 + dev[1]).astype(F32)
        for s in range(4):
            for k in range(2):
                info = metas[j, s, k]
                named = jnp.zeros((16, TOK), F32)
                for i in range(TOP):
                    named = named + jnp.where(info[i : i + 1, :] == expert, 1.0, 0.0)
                earlier = jnp.dot(named.astype(BF), before, preferred_element_type=F32)
                pos[j, s, k] = jnp.where(named > 0.5, earlier, -1.0)

    def gather(j, par, r):
        a, b, c = axes[j]
        w = WIDTH[r][j]
        for h in range(2):
            s = 2 * h + (par + b + c) % 2
            rows = T[j][r][s].reshape(2 * TOK, w)
            main = jnp.dot(one_hot(j, s, r == 1, False), rows, preferred_element_type=F32)
            S[j][r][:, :, par, h] = main.astype(BF).reshape(4, 4, 16, w)

    def gather_tails(j):
        tails = []
        for r in range(2):
            w = WIDTH[r][j]
            rows = jnp.zeros((TAILS, w), F32)
            for s in range(4):
                picked = T[j][r][s].reshape(2 * TOK, w)
                rows = rows + jnp.dot(one_hot(j, s, r == 1, True), picked, preferred_element_type=F32)
            left = START[r][j] - TAIL_START[j]
            right = TAIL_WIDTH[j] - w - left
            rows = [rows]
            if left:
                rows = [jnp.zeros((TAILS, left), F32)] + rows
            if right:
                rows = rows + [jnp.zeros((TAILS, right), F32)]
            tails.append(jnp.concatenate(rows, axis=1).reshape(16, 8, TAIL_WIDTH[j]))
        ST[j][...] = jnp.concatenate(tails, axis=1).astype(BF).reshape(4, 4, 16, TAIL_WIDTH[j])

    def along_b(j, par, r):
        a, b, c = axes[j]
        for d in (2, 1, 3):
            t = (b + d) % 4
            dev = device(j, a, t, c, core)
            src, dst = S[j][r].at[t, :, par], R[j][r].at[b, :, par]
            go(remote(src, dst, p2_s.at[j, par, d, r], p2_r.at[j, par, b, r], dev))

    def along_c(j, par, d, r, main):
        a, b, c = axes[j]
        s = (b + d) % 4
        dst = canon(j, XG, (r,), par, s, c, cols_of(r, j))
        for dc in (2, 1, 3):
            t = (c + dc) % 4
            dev = device(j, a, b, t, core)
            go(remote(main.at[s, t, par], dst, p3_s.at[j, par, d, dc, r], p3_r.at[j, par, c, s, r], dev))
        pltpu.make_async_copy(main.at[s, c, par], dst, locp.at[j, par, d, r]).start()

    def depart(j, par, r):
        along_b(j, par, r)
        along_c(j, par, 0, r, S[j][r])

    def tails_along_b(j):
        a, b, c = axes[j]
        for d in (2, 1, 3):
            t = (b + d) % 4
            dev = device(j, a, t, c, core)
            go(remote(ST[j].at[t], RT[j].at[b], p2t_s.at[j, d], p2t_r.at[j, b], dev))

    def tails_along_c(j, d, tail):
        a, b, c = axes[j]
        s = (b + d) % 4
        for dc in (2, 1, 3):
            t = (c + dc) % 4
            dev = device(j, a, b, t, core)
            go(remote(tail.at[s, t], FT[j].at[c, s], p3t_s.at[j, d, dc], p3t_r.at[j, c, s], dev))
        pltpu.make_async_copy(tail.at[s, c], FT[j].at[c, s], loct.at[j, d]).start()

    def pass_on(par, r):
        for d in (1, 3, 2):
            for j in range(3):
                s = (axes[j][1] + d) % 4
                got(R[j][r].at[s, :, par], p2_r.at[j, par, s, r])
                along_c(j, par, d, r, R[j][r])

    def pass_tails():
        for d in (1, 3, 2):
            for j in range(3):
                s = (axes[j][1] + d) % 4
                got(RT[j].at[s], p2t_r.at[j, s])
                tails_along_c(j, d, RT[j])

    def arrive(par, r):
        for j in range(3):
            a, b, c = axes[j]
            for db in (0, 1, 3, 2):
                s = (b + db) % 4
                landed(canon(j, XG, (r,), par, s, c, cols_of(r, j)), locp.at[j, par, db, r])
                for dc in (1, 2, 3):
                    t = (c + dc) % 4
                    got(canon(j, XG, (r,), par, s, t, cols_of(r, j)), p3_r.at[j, par, t, s, r])

    def arrive_tails():
        for j in range(3):
            a, b, c = axes[j]
            for db in range(4):
                s = (b + db) % 4
                landed(FT[j].at[c, s], loct.at[j, db])
                for dc in (1, 2, 3):
                    t = (c + dc) % 4
                    got(FT[j].at[t, s], p3t_r.at[j, t, s])
            rows = FT[j][...].reshape(256, TAIL_WIDTH[j])
            for r in range(2):
                picked = jnp.dot(tail_perm(j, r), rows, preferred_element_type=F32).astype(BF)
                left = START[r][j] - TAIL_START[j]
                XT[r, :, cols_of(r, j)] = picked[:, left : left + WIDTH[r][j]]

    first, size = (0, MAIN_A + TAILS), (MAIN_A + TAILS, MAIN_A)

    def rows_of(r, par):
        main = XG[r, par].reshape(MAIN_A, D)
        return jnp.concatenate([main, XT[r]], axis=0) if par == 0 else main

    def before_hidden():
        def tile_of(i, carry):
            cols = tile(i)
            rows = rows_of(0, 1)
            KEEP[0][:, :, cols] = jnp.dot(rows, WG[:, cols], preferred_element_type=F32).reshape(2, 256, 256)
            KEEP[1][:, :, cols] = jnp.dot(rows, WU[:, cols], preferred_element_type=F32).reshape(2, 256, 256)
            return carry

        lax.fori_loop(0, FF // 256, tile_of, 0)

    def forward(par):
        span = pl.ds(first[par], size[par])

        def hidden_tile(i, carry):
            cols = tile(i)
            if par == 0:
                rows = rows_of(0, par)
                gate_pre = jnp.dot(rows, WG[:, cols], preferred_element_type=F32)
                up_pre = jnp.dot(rows, WU[:, cols], preferred_element_type=F32)
            else:
                gate_pre = KEEP[0][:, :, cols].reshape(MAIN_A, 256)
                up_pre = KEEP[1][:, :, cols].reshape(MAIN_A, 256)
            hidden_grad = across(rows_of(1, par), WD[cols, :])
            logistic = jax.nn.sigmoid(gate_pre)
            silu_gate = gate_pre * logistic
            HID[span, cols] = (silu_gate * up_pre).astype(BF)
            UG[span, cols] = (hidden_grad * silu_gate).astype(BF)
            GG[span, cols] = (hidden_grad * up_pre * logistic * (1.0 + gate_pre * (1.0 - logistic))).astype(BF)
            return carry

        lax.fori_loop(0, FF // 256, hidden_tile, 0)

        def slot_tile(i, carry):
            cols = tile(i)
            rows = (across(GG[span, :], WG[cols, :]) + across(UG[span, :], WU[cols, :])).astype(BF)
            SG[par, :, :, :, :, :, :, cols] = rows[:MAIN_A].reshape(2, 2, 2, 2, 2, 16, 256)
            if par == 0:
                SGT[:, cols] = rows[MAIN_A:]
            return carry

        ready = 0
        for j in range(3):
            stop = -(-(START[par][j] + WIDTH[par][j]) // 256)
            lax.fori_loop(ready, stop, slot_tile, 0)
            ready = stop
            back_c(par, j)

    def in_tile(i, carry):
        cols = tile(i)
        parts = [XG[0, 0, :, :, :, :, :, :, cols].reshape(MAIN_A, 256), XT[0, :, cols]]
        rows = jnp.concatenate(parts + [XG[0, 1, :, :, :, :, :, :, cols].reshape(MAIN_A, 256)], axis=0)
        WG[cols, :] = over_rows(rows, GG[...]).astype(BF)
        WU[cols, :] = over_rows(rows, UG[...]).astype(BF)
        return carry

    def down_tile(i, carry):
        cols = tile(i)
        rows = jnp.concatenate([rows_of(1, 0), rows_of(1, 1)], axis=0)
        WD[cols, :] = over_rows(HID[:, cols], rows).astype(BF)
        return carry

    def back_c(par, j):
        a, b, c = axes[j]
        for d in (2, 1, 3):
            t = (c + d) % 4
            dev = device(j, a, b, t, core)
            for bl in range(2):
                if j == 0:
                    at = (par, t // 2, t % 2, slice(None), bl, slice(None))
                elif j == 1:
                    at = (par, slice(None), bl, slice(None), (par + bl + t) % 2, t // 2)
                else:
                    at = (par, slice(None), (par + bl + t) % 2, t // 2, t % 2, slice(None))
                src = SG.at[at + (slice(None), cols_of(par, j))]
                go(remote(src, R1[j][par].at[c, bl], r1_s.at[j, par, d, bl], r1_r.at[j, par, c, bl], dev))
        if par == 0:
            lo, hi = TAIL_START[j], TAIL_START[j] + TAIL_WIDTH[j] - HALF
            rows = jnp.dot(tail_spread(j, 0), SGT[:, lo : lo + HALF], preferred_element_type=F32)
            rows = rows + jnp.dot(tail_spread(j, 1), SGT[:, hi : hi + HALF], preferred_element_type=F32)
            ST2[j][...] = rows.astype(BF).reshape(4, 4, 16, HALF)
            for d in (2, 1, 3):
                t = (c + d) % 4
                dev = device(j, a, b, t, core)
                go(remote(ST2[j].at[t], RT1[j].at[c], r1t_s.at[j, d], r1t_r.at[j, c], dev))
        back_b(j, par, 0, lambda t: canon(j, SG, (), par, t, c, cols_of(par, j)), ST2[j].at[c])

    def back_b(j, par, d, main, tail):
        a, b, c = axes[j]
        s = (c + d) % 4
        for db in (2, 1, 3):
            t = (b + db) % 4
            dev = device(j, a, t, c, core)
            go(remote(main(t), R2[j][par].at[b, s], r2_s.at[j, par, d, db], r2_r.at[j, par, b, s], dev))
            if par == 0:
                go(remote(tail.at[t], RT2[j].at[b, s], r2t_s.at[j, d, db], r2t_r.at[j, b, s], dev))
        pltpu.make_async_copy(main(b), R2[j][par].at[b, s], l2.at[j, par, d]).start()
        if par == 0:
            pltpu.make_async_copy(tail.at[b], RT2[j].at[b, s], l2t.at[j, d]).start()

    def pass_back(par):
        for d in (1, 3, 2):
            for j in range(3):
                s = (axes[j][2] + d) % 4
                for bl in range(2):
                    got(R1[j][par].at[s, bl], r1_r.at[j, par, s, bl])
                if par == 0:
                    got(RT1[j].at[s], r1t_r.at[j, s])

                def main(t, j=j, s=s):
                    if j == 2:
                        return R1[j][par].at[s, t % 2, :, t // 2]
                    return R1[j][par].at[s, t % 2, t // 2]

                back_b(j, par, d, main, RT1[j].at[s])

    def returned(par, j):
        a, b, c = axes[j]
        for dc in (0, 1, 3, 2):
            s = (c + dc) % 4
            landed(R2[j][par].at[b, s], l2.at[j, par, dc])
            for db in (1, 2, 3):
                t = (b + db) % 4
                got(R2[j][par].at[t, s], r2_r.at[j, par, t, s])

    def tails_returned(j):
        a, b, c = axes[j]
        for dc in (0, 1, 3, 2):
            s = (c + dc) % 4
            landed(RT2[j].at[b, s], l2t.at[j, dc])
            for db in (1, 2, 3):
                t = (b + db) % 4
                got(RT2[j].at[t, s], r2t_r.at[j, t, s])

    def prepare(par, j):
        a, b, c = axes[j]
        left, w = START[par][j] - TAIL_START[j], WIDTH[par][j]
        tails = RT2[j][...].reshape(256, HALF)
        for h in range(2):
            s = 2 * h + (par + b + c) % 2
            pick, low, high = [], [], []
            for k in range(2):
                who = (core + k) % 2
                at = pos[j, s, who][:, None, :]
                row = iota((16, 16, TOK), 1)
                hit = at * 2.0 + who.astype(F32) == row.astype(F32)
                pick.append(jnp.where(hit, 1.0, 0.0).reshape(256, TOK))
                hit = (at == 8.0) & (row == 2 * s + who)
                low.append(jnp.where(hit, 1.0, 0.0).reshape(256, TOK))
                hit = (at == 8.0) & (row == 8 + 2 * s + who)
                high.append(jnp.where(hit, 1.0, 0.0).reshape(256, TOK))
            pick, low, high = (jnp.concatenate(p, axis=1).astype(BF) for p in (pick, low, high))
            PK[j, h] = pick
            both = [over_rows(low, tails), over_rows(high, tails)[:, 2 * HALF - TAIL_WIDTH[j] :]]
            KEEP[j][h, :, :w] = jnp.concatenate(both, axis=1)[:, left : left + w]

    def combine(par):
        swaps = []
        for j in range(3):
            returned(par, j)
            w = WIDTH[par][j]
            for h in range(2):
                total = KEEP[j][h, :, :w] + over_rows(PK[j, h], R2[j][par][:, :, h].reshape(256, w))
                KEEP[j][h, :TOK, :w] = total[:TOK]
                T[j][par][h, 0] = total[TOK:].astype(BF)
                mine, theirs = T[j][par].at[h, 0], T[j][par].at[h, 1]
                cp = remote(mine, theirs, ps_s.at[j, 2 * par + h], ps_r.at[j, 2 * par + h], sib)
                cp.start()
                swaps.append(cp)
        for j in range(3):
            a, b, c = axes[j]
            w = WIDTH[par][j]
            for h in range(2):
                s = 2 * h + (par + b + c) % 2
                swaps[2 * j + h].wait_send()
                got(T[j][par].at[h, 1], ps_r.at[j, 2 * par + h])
                total = KEEP[j][h, :TOK, :w] + T[j][par][h, 1].astype(F32)

                @pl.when(s == a)
                def _():
                    OWN[:, cols_of(par, j)] = total

                @pl.when(s != a)
                def _():
                    T[j][par][h, 0] = total.astype(BF)
                    to_line(j, par, h, s).start()

    def to_line(j, par, h, s):
        a, b, c = axes[j]
        dst = T[j][par].at[2 + a // 2, a % 2]
        return remote(T[j][par].at[h, 0], dst, q_s.at[j, 2 * par + h], q_r.at[j, a], device(j, s, b, c, core))

    for j in range(3):
        a, b, c = axes[j]
        landed(metas.at[j, a, core], locm.at[j])
        for s in range(4):
            got(metas.at[j, s, 1 - core], msib_r.at[j, s])
        find_slots(j)
    def complete(j, r):
        landed(T[j][r].at[axes[j][0], core], loc.at[j, r])
        for s in range(4):
            got(T[j][r].at[s, 1 - core], sib_r.at[j, s, r])

    for j in range(3):
        complete(j, 0)
        gather(j, 0, 0)
        depart(j, 0, 0)
    for d in (1, 3):
        rows_across(d, 1)
    second_hop(1)
    pass_on(0, 0)
    rows_across(2, 1)
    for j in range(3):
        complete(j, 1)
        gather(j, 0, 1)
        depart(j, 0, 1)
    for j in range(3):
        gather_tails(j)
        tails_along_b(j)
        tails_along_c(j, 0, ST[j])
    for j in range(3):
        for r in range(2):
            gather(j, 1, r)
    for cp in early:
        cp.wait_send()
    pl.semaphore_signal(done, inc=1, device_id=sib, device_id_type=MESH)
    pass_on(0, 1)
    pass_tails()
    for r in range(2):
        for j in range(3):
            depart(j, 1, r)
    arrive(0, 0)
    arrive(0, 1)
    arrive_tails()
    for i, (src, dst) in enumerate(weights):
        pltpu.make_async_copy(src.at[0], dst, wsem.at[i]).wait()
    forward(0)
    pass_on(1, 0)
    pass_on(1, 1)
    pass_back(0)
    arrive(1, 0)
    before_hidden()
    arrive(1, 1)
    forward(1)
    pl.semaphore_wait(done, 1)
    for j in range(3):
        tails_returned(j)
        prepare(0, j)
    combine(0)
    for j in range(3):
        prepare(1, j)
    pass_back(1)
    lax.fori_loop(0, 8, in_tile, 0)
    lax.fori_loop(0, 3, down_tile, 0)
    combine(1)
    for m in range(2):

        @pl.when((x + y + z) % 2 == m)
        def _():
            for j in range(3):
                a = axes[j][0]
                total = OWN[:, cols_of(m, j)]
                for d in (1, 3, 2):
                    s = (a + d) % 4
                    part = T[j][m].at[2 + s // 2, s % 2]
                    got(part, q_r.at[j, s])
                    total = total + part[...].astype(F32)
                out[:, cols_of(m, j)] = total.astype(BF)

    for cp in sends:
        cp.wait_send()
    for j in range(3):
        a, b, c = axes[j]
        for i in range(4):
            s = 2 * (i % 2) + (i // 2 + b + c) % 2

            @pl.when(s != a)
            def _():
                to_line(j, i // 2, i % 2, s).wait_send()


def run(tokens, out_grad, ids, gates, gate_weight, up_weight, down_weight):
    dma = pltpu.SemaphoreType.DMA
    vm = pltpu.VMEM
    any_spec = pl.BlockSpec(memory_space=pl.ANY)
    vm_spec = pl.BlockSpec(memory_space=pltpu.VMEM)
    shape = jax.ShapeDtypeStruct
    both = [WIDTH[i][j] for j in range(3) for i in range(2)]
    scratch = [vm((4, 2, TOK, w), BF) for w in both]
    scratch += [vm((4, 4, 2, 2, 16, w), BF) for w in both]
    scratch += [vm((4, 4, 2, 16, w), BF) for w in both]
    scratch += [vm((4, 4, 16, w), BF) for w in TAIL_WIDTH] * 2
    scratch += [vm((4, 4, 16, HALF), BF)] * 6
    scratch += [vm((2, 2 * TOK, 768), F32)] * 3
    scratch += [vm((3, 2, 256, 256), BF), vm((TOK, D), F32)]
    scratch += [vm((2, 2, 2, 2, 2, 2, 2, 16, D), BF), vm((2, TAILS, D), BF)]
    scratch += [vm((2, 2, 2, 2, 2, 2, 16, D), BF), vm((TAILS, D), BF)]
    scratch += [vm((ROWS, FF), BF)] * 3
    scratch += [vm((2 * TOP, TOK), F32)] + [vm((3, 4, 2, 16, TOK), F32)] * 2
    scratch += [dma((3, 4, 2))] * 4 + [dma((3, 4))] * 4 + [dma((3, 2)), dma((3,))]
    scratch += [dma((3, 2, 4, 2))] * 2 + [dma((3, 4))] * 2 + [dma((3, 2, 4, 4, 2))] * 2 + [dma((3, 4, 4))] * 2
    scratch += [dma((3, 2, 4, 2)), dma((3, 4))]
    scratch += [dma((3, 2, 4, 2))] * 2 + [dma((3, 4))] * 2 + [dma((3, 2, 4, 4))] * 2 + [dma((3, 4, 4))] * 2
    scratch += [dma((3, 2, 4)), dma((3, 4))]
    scratch += [dma((3, 4))] * 4 + [dma((3,))] + [pltpu.SemaphoreType.REGULAR]
    outs = [vm((TOK, D), BF), vm((1, D, FF), BF), vm((1, D, FF), BF), vm((1, FF, D), BF)]
    outs += [shape((4, 4, 2, 2, 16, w), BF) for w in both]
    outs += [shape((4, 2, 2, 2, 16, w), BF) for w in both]
    outs += [shape((4, 4, 16, w), BF) for w in TAIL_WIDTH] + [shape((4, 4, 16, HALF), BF)] * 3
    return pl.pallas_call(
        kernel,
        name="experts",
        out_shape=outs,
        in_specs=[any_spec] * 2 + [vm_spec] * 2 + [any_spec] * 3,
        out_specs=[vm_spec] * 4 + [any_spec] * 18,
        scratch_shapes=scratch,
        compiler_params=pltpu.CompilerParams(collective_id=0, has_side_effects=True, vmem_limit_bytes=52 << 20),
    )(tokens, out_grad, ids, gates, gate_weight, up_weight, down_weight)[:4]


def body(tokens, out_grad, expert_ids, gates, gate_weight, up_weight, down_weight):
    return tuple(run(tokens, out_grad, expert_ids.T, gates.T, gate_weight, up_weight, down_weight))


def solution(mesh):
    whole = ("node", "local")
    two, three = P(whole, None), P(whole, None, None)
    return jax.shard_map(
        body,
        mesh=mesh,
        in_specs=(two, two, two, two, three, three, three),
        out_specs=(two, three, three, three),
        check_vma=False,
    )
```

```python
import functools

import jax
import jax.numpy as jnp
from jax import lax
from jax.experimental import pallas as pl
from jax.experimental.pallas import tpu as pltpu
from jax.sharding import PartitionSpec as P

MESH = pl.DeviceIdType.MESH
BF, F32 = jnp.bfloat16, jnp.float32
D, FF, TOK, TOP, SLOTS = 2048, 768, 128, 8, 9
WIDTH = ((640, 768, 640), (640, 640, 768))
START = ((0, 640, 1408), (0, 640, 1280))
TAIL_WIDTH = (640, 768, 768)
TAIL_START = (0, 640, 1280)
HALF = 384
ROWS = 1152
MAIN_A, TAILS = 512, 128


def place():
    node, local = lax.axis_index("node"), lax.axis_index("local")
    return local // 2, (node % 8) // 2, (node // 8) * 2 + local % 2, node % 2


def order(j, x, y, z):
    return ((x, y, z), (y, z, x), (z, x, y))[j]


def device(j, a, b, c, core):
    x, y, z = ((a, b, c), (c, a, b), (b, c, a))[j]
    return ((z // 2) * 8 + y * 2 + core, x * 2 + z % 2)


def canon(j, ref, lead, par, b, c, cols):
    q = (par + b + c) % 2
    every = slice(None)
    if j == 0:
        at = (par, c // 2, c % 2, b // 2, b % 2, every)
    elif j == 1:
        at = (par, b // 2, b % 2, every, q, c // 2)
    else:
        at = (par, every, q, c // 2, c % 2, b // 2)
    return ref.at[lead + at + (every, cols)]


def remote(src, dst, ssem, rsem, dev):
    return pltpu.make_async_remote_copy(
        src_ref=src, dst_ref=dst, send_sem=ssem, recv_sem=rsem, device_id=dev, device_id_type=MESH
    )


def greet(partners):
    barrier = pltpu.get_barrier_semaphore()
    for dev in partners:
        pl.semaphore_signal(barrier, inc=1, device_id=dev, device_id_type=MESH)
    pl.semaphore_wait(barrier, len(partners))


def partners_of(x, y, z, core):
    out = [device(0, x, y, z, 1 - core)]
    for d in (1, 2, 3):
        out.append(device(0, (x + d) % 4, y, z, core))
        out.append(device(0, x, (y + d) % 4, z, core))
        out.append(device(0, x, y, (z + d) % 4, core))
    return out


def iota(shape, dim):
    return lax.broadcasted_iota(jnp.int32, shape, dim)


def tail_perm(j, array):
    row, col = iota((128, 256), 0), iota((128, 256), 1)
    core, x, y, z = row % 2, (row // 2) % 4, (row // 8) % 4, row // 32
    a, b, c = order(j, x, y, z)
    want = c * 64 + b * 16 + array * 8 + a * 2 + core
    return (col == want).astype(F32).astype(BF)


def tail_spread(j, half):
    row, col = iota((256, 128), 0), iota((256, 128), 1)
    c, b, h, a, core = row // 64, (row // 16) % 4, (row // 8) % 2, (row // 2) % 4, row % 2
    x, y, z = ((a, b, c), (c, a, b), (b, c, a))[j]
    return ((col == z * 32 + y * 8 + x * 2 + core) & (h == half)).astype(F32).astype(BF)


def over_rows(left, right):
    return lax.dot_general(left, right, (((0,), (0,)), ((), ())), preferred_element_type=F32)


def across(left, right):
    return lax.dot_general(left, right, (((1,), (1,)), ((), ())), preferred_element_type=F32)


def tile(i):
    return pl.ds(pl.multiple_of(i * 256, 256), 256)


def by_two(refs):
    return tuple(refs[2 * j : 2 * j + 2] for j in range(3))


def kernel(tok, grad, ids, gates, gate_w, up_w, down_w, out, gate_out, up_out, down_out, *rest):
    R, R1, RT, RT1, scr = by_two(rest[:6]), by_two(rest[6:12]), rest[12:15], rest[15:18], rest[18:]
    T, S, R2 = (by_two(scr[6 * i : 6 * i + 6]) for i in range(3))
    ST, FT, ST2, RT2, KEEP = (scr[18 + 3 * i : 21 + 3 * i] for i in range(5))
    PK, OWN, XG, XT, SG, SGT, HID, GG, UG, meta, metas, pos = scr[33:45]
    (ag_s, ag_r, sib_s, sib_r, mag_s, mag_r, msib_s, msib_r, loc, locm,
     p2_s, p2_r, p2t_s, p2t_r, p3_s, p3_r, p3t_s, p3t_r, locp, loct,
     r1_s, r1_r, r1t_s, r1t_r, r2_s, r2_r, r2t_s, r2t_r, l2, l2t,
     ps_s, ps_r, q_s, q_r, wsem, done) = scr[45:]
    WG, WU, WD = gate_out.at[0], up_out.at[0], down_out.at[0]
    x, y, z, core = place()
    axes = [order(j, x, y, z) for j in range(3)]
    sib = device(0, x, y, z, 1 - core)
    weights = ((gate_w, WG), (up_w, WU), (down_w, WD))
    for i, (src, dst) in enumerate(weights):
        pltpu.make_async_copy(src.at[0], dst, wsem.at[i]).start()
    meta[:TOP] = ids[...].astype(F32)
    meta[TOP:] = gates[...].astype(F32)
    greet(partners_of(x, y, z, core))
    ins = (tok, grad)
    sends, early = [], []

    def go(cp, kept=sends):
        cp.start()
        kept.append(cp)

    def drain(count):
        for cp in sends[:count]:
            cp.wait_send()
        del sends[:count]

    def got(ref, rsem):
        remote(ref, ref, ag_s.at[0, 0, 0], rsem, sib).wait_recv()

    def landed(ref, sem):
        pltpu.make_async_copy(ref, ref, sem).wait()

    def cols_of(i, j):
        return pl.ds(START[i][j], WIDTH[i][j])

    for j in range(3):
        a, b, c = axes[j]
        for d in (2, 1, 3):
            dev = device(j, (a + d) % 4, b, c, core)
            go(remote(meta, metas.at[j, a, core], mag_s.at[j, d], mag_r.at[j, a], dev))
    def to_lines(r):
        for d in (1, 3):
            for j in range(3):
                a, b, c = axes[j]
                dev = device(j, (a + d) % 4, b, c, core)
                src = ins[r].at[:, cols_of(r, j)]
                go(remote(src, T[j][r].at[a, core], ag_s.at[j, d, r], ag_r.at[j, a, r], dev))

    def metas_across(d):
        for j in range(3):
            s = (axes[j][0] + d) % 4
            m = metas.at[j, s, core]
            got(m, mag_r.at[j, s])
            go(remote(m, m, msib_s.at[j, s], msib_r.at[j, s], sib))

    def rows_across(d, r):
        for j in range(3):
            s = (axes[j][0] + d) % 4
            t = T[j][r].at[s, core]
            got(t, ag_r.at[j, s, r])
            go(remote(t, t, sib_s.at[j, s, r], sib_r.at[j, s, r], sib), early)

    def second_hop(r):
        for j in range(3):
            a, b, c = axes[j]
            way = 1 - 2 * core
            t = T[j][r].at[(a - way) % 4, core]
            dev = device(j, (a + way) % 4, b, c, core)
            go(remote(t, t, ag_s.at[j, 2, r], ag_r.at[j, (a - way) % 4, r], dev), early)

    to_lines(0)
    for j in range(3):
        a, b, c = axes[j]
        go(remote(meta, metas.at[j, a, core], msib_s.at[j, a], msib_r.at[j, a], sib))
        pltpu.make_async_copy(meta, metas.at[j, a, core], locm.at[j]).start()
        for r in range(2):
            src = ins[r].at[:, cols_of(r, j)]
            go(remote(src, T[j][r].at[a, core], sib_s.at[j, a, r], sib_r.at[j, a, r], sib))
            pltpu.make_async_copy(src, T[j][r].at[a, core], loc.at[j, r]).start()
    for d in (1, 3):
        metas_across(d)
        rows_across(d, 0)
    second_hop(0)
    to_lines(1)
    metas_across(2)
    rows_across(2, 0)

    before = (iota((TOK, TOK), 0) < iota((TOK, TOK), 1)).astype(F32).astype(BF)

    def one_hot(j, s, gate, last):
        a = axes[j][0]
        e = iota((16, 1), 0)
        dev = device(j, a, e // 4, e % 4, core)
        expert = (dev[0] * 8 + dev[1]).astype(F32)
        parts = []
        for k in range(2):
            info = metas[j, s, k]
            value = jnp.ones((16, TOK), F32)
            if gate:
                value = jnp.zeros((16, TOK), F32)
                for i in range(TOP):
                    hit = info[i : i + 1, :] == expert
                    value = value + jnp.where(hit, info[TOP + i : TOP + i + 1, :], 0.0)
            at = pos[j, s, k][:, None, :]
            if last:
                hit = (at == 8.0) & (iota((16, 8, TOK), 1) == 2 * s + k)
            else:
                hit = at * 2.0 + k == iota((16, 16, TOK), 1).astype(F32)
            parts.append(jnp.where(hit, value[:, None, :], 0.0).reshape(128 if last else 256, TOK))
        return jnp.concatenate(parts, axis=1).astype(BF)

    def find_slots(j):
        a = axes[j][0]
        e = iota((16, 1), 0)
        dev = device(j, a, e // 4, e % 4, core)
        expert = (dev[0] * 8 + dev[1]).astype(F32)
        for s in range(4):
            for k in range(2):
                info = metas[j, s, k]
                named = jnp.zeros((16, TOK), F32)
                for i in range(TOP):
                    named = named + jnp.where(info[i : i + 1, :] == expert, 1.0, 0.0)
                earlier = jnp.dot(named.astype(BF), before, preferred_element_type=F32)
                pos[j, s, k] = jnp.where(named > 0.5, earlier, -1.0)

    def gather(j, par, r):
        a, b, c = axes[j]
        w = WIDTH[r][j]
        for h in range(2):
            s = 2 * h + (par + b + c) % 2
            rows = T[j][r][s].reshape(2 * TOK, w)
            main = jnp.dot(one_hot(j, s, r == 1, False), rows, preferred_element_type=F32)
            S[j][r][:, :, par, h] = main.astype(BF).reshape(4, 4, 16, w)

    def gather_tails(j):
        tails = []
        for r in range(2):
            w = WIDTH[r][j]
            rows = jnp.zeros((TAILS, w), F32)
            for s in range(4):
                picked = T[j][r][s].reshape(2 * TOK, w)
                rows = rows + jnp.dot(one_hot(j, s, r == 1, True), picked, preferred_element_type=F32)
            left = START[r][j] - TAIL_START[j]
            right = TAIL_WIDTH[j] - w - left
            rows = [rows]
            if left:
                rows = [jnp.zeros((TAILS, left), F32)] + rows
            if right:
                rows = rows + [jnp.zeros((TAILS, right), F32)]
            tails.append(jnp.concatenate(rows, axis=1).reshape(16, 8, TAIL_WIDTH[j]))
        ST[j][...] = jnp.concatenate(tails, axis=1).astype(BF).reshape(4, 4, 16, TAIL_WIDTH[j])

    def along_b(j, par, r):
        a, b, c = axes[j]
        for d in (2, 1, 3):
            t = (b + d) % 4
            dev = device(j, a, t, c, core)
            src, dst = S[j][r].at[t, :, par], R[j][r].at[b, :, par]
            go(remote(src, dst, p2_s.at[j, par, d, r], p2_r.at[j, par, b, r], dev))

    def along_c(j, par, d, r, main):
        a, b, c = axes[j]
        s = (b + d) % 4
        dst = canon(j, XG, (r,), par, s, c, cols_of(r, j))
        for dc in (2, 1, 3):
            t = (c + dc) % 4
            dev = device(j, a, b, t, core)
            go(remote(main.at[s, t, par], dst, p3_s.at[j, par, d, dc, r], p3_r.at[j, par, c, s, r], dev))
        pltpu.make_async_copy(main.at[s, c, par], dst, locp.at[j, par, d, r]).start()

    def depart(j, par, r):
        along_b(j, par, r)
        along_c(j, par, 0, r, S[j][r])

    def tails_along_b(j):
        a, b, c = axes[j]
        for d in (2, 1, 3):
            t = (b + d) % 4
            dev = device(j, a, t, c, core)
            go(remote(ST[j].at[t], RT[j].at[b], p2t_s.at[j, d], p2t_r.at[j, b], dev))

    def tails_along_c(j, d, tail):
        a, b, c = axes[j]
        s = (b + d) % 4
        for dc in (2, 1, 3):
            t = (c + dc) % 4
            dev = device(j, a, b, t, core)
            go(remote(tail.at[s, t], FT[j].at[c, s], p3t_s.at[j, d, dc], p3t_r.at[j, c, s], dev))
        pltpu.make_async_copy(tail.at[s, c], FT[j].at[c, s], loct.at[j, d]).start()

    def pass_on(par, r):
        for d in (1, 3, 2):
            for j in range(3):
                s = (axes[j][1] + d) % 4
                got(R[j][r].at[s, :, par], p2_r.at[j, par, s, r])
                along_c(j, par, d, r, R[j][r])

    def pass_tails():
        for d in (1, 3, 2):
            for j in range(3):
                s = (axes[j][1] + d) % 4
                got(RT[j].at[s], p2t_r.at[j, s])
                tails_along_c(j, d, RT[j])

    def arrive(par, r):
        for j in range(3):
            a, b, c = axes[j]
            for db in (0, 1, 3, 2):
                s = (b + db) % 4
                landed(canon(j, XG, (r,), par, s, c, cols_of(r, j)), locp.at[j, par, db, r])
                for dc in (1, 2, 3):
                    t = (c + dc) % 4
                    got(canon(j, XG, (r,), par, s, t, cols_of(r, j)), p3_r.at[j, par, t, s, r])

    def arrive_tails():
        for j in range(3):
            a, b, c = axes[j]
            for db in range(4):
                s = (b + db) % 4
                landed(FT[j].at[c, s], loct.at[j, db])
                for dc in (1, 2, 3):
                    t = (c + dc) % 4
                    got(FT[j].at[t, s], p3t_r.at[j, t, s])
            rows = FT[j][...].reshape(256, TAIL_WIDTH[j])
            for r in range(2):
                picked = jnp.dot(tail_perm(j, r), rows, preferred_element_type=F32).astype(BF)
                left = START[r][j] - TAIL_START[j]
                XT[r, :, cols_of(r, j)] = picked[:, left : left + WIDTH[r][j]]

    first, size = (0, MAIN_A + TAILS), (MAIN_A + TAILS, MAIN_A)

    def rows_of(r, par):
        main = XG[r, par].reshape(MAIN_A, D)
        return jnp.concatenate([main, XT[r]], axis=0) if par == 0 else main

    def before_hidden():
        def tile_of(i, carry):
            cols = tile(i)
            rows = rows_of(0, 1)
            KEEP[0][:, :, cols] = jnp.dot(rows, WG[:, cols], preferred_element_type=F32).reshape(2, 256, 256)
            KEEP[1][:, :, cols] = jnp.dot(rows, WU[:, cols], preferred_element_type=F32).reshape(2, 256, 256)
            return carry

        lax.fori_loop(0, FF // 256, tile_of, 0)

    def forward(par, meanwhile=lambda: None):
        span = pl.ds(first[par], size[par])

        def hidden_tile(i, carry):
            cols = tile(i)
            if par == 0:
                rows = rows_of(0, par)
                gate_pre = jnp.dot(rows, WG[:, cols], preferred_element_type=F32)
                up_pre = jnp.dot(rows, WU[:, cols], preferred_element_type=F32)
            else:
                gate_pre = KEEP[0][:, :, cols].reshape(MAIN_A, 256)
                up_pre = KEEP[1][:, :, cols].reshape(MAIN_A, 256)
            hidden_grad = across(rows_of(1, par), WD[cols, :])
            logistic = jax.nn.sigmoid(gate_pre)
            silu_gate = gate_pre * logistic
            HID[span, cols] = (silu_gate * up_pre).astype(BF)
            UG[span, cols] = (hidden_grad * silu_gate).astype(BF)
            GG[span, cols] = (hidden_grad * up_pre * logistic * (1.0 + gate_pre * (1.0 - logistic))).astype(BF)
            return carry

        lax.fori_loop(0, FF // 256, hidden_tile, 0)
        meanwhile()

        def slot_tile(i, carry):
            cols = tile(i)
            rows = (across(GG[span, :], WG[cols, :]) + across(UG[span, :], WU[cols, :])).astype(BF)
            SG[par, :, :, :, :, :, :, cols] = rows[:MAIN_A].reshape(2, 2, 2, 2, 2, 16, 256)
            if par == 0:
                SGT[:, cols] = rows[MAIN_A:]
            return carry

        ready = 0
        for j in range(3):
            stop = -(-(START[par][j] + WIDTH[par][j]) // 256)
            lax.fori_loop(ready, stop, slot_tile, 0)
            ready = stop
            back_c(par, j)

    def in_tile(i, carry):
        cols = tile(i)
        parts = [XG[0, 0, :, :, :, :, :, :, cols].reshape(MAIN_A, 256), XT[0, :, cols]]
        rows = jnp.concatenate(parts + [XG[0, 1, :, :, :, :, :, :, cols].reshape(MAIN_A, 256)], axis=0)
        WG[cols, :] = over_rows(rows, GG[...]).astype(BF)
        WU[cols, :] = over_rows(rows, UG[...]).astype(BF)
        return carry

    def down_tile(i, carry):
        cols = tile(i)
        rows = jnp.concatenate([rows_of(1, 0), rows_of(1, 1)], axis=0)
        WD[cols, :] = over_rows(HID[:, cols], rows).astype(BF)
        return carry

    def back_c(par, j):
        a, b, c = axes[j]
        for d in (2, 1, 3):
            t = (c + d) % 4
            dev = device(j, a, b, t, core)
            for bl in range(2):
                if j == 0:
                    at = (par, t // 2, t % 2, slice(None), bl, slice(None))
                elif j == 1:
                    at = (par, slice(None), bl, slice(None), (par + bl + t) % 2, t // 2)
                else:
                    at = (par, slice(None), (par + bl + t) % 2, t // 2, t % 2, slice(None))
                src = SG.at[at + (slice(None), cols_of(par, j))]
                go(remote(src, R1[j][par].at[c, bl], r1_s.at[j, par, d, bl], r1_r.at[j, par, c, bl], dev))
        if par == 0:
            lo, hi = TAIL_START[j], TAIL_START[j] + TAIL_WIDTH[j] - HALF
            rows = jnp.dot(tail_spread(j, 0), SGT[:, lo : lo + HALF], preferred_element_type=F32)
            rows = rows + jnp.dot(tail_spread(j, 1), SGT[:, hi : hi + HALF], preferred_element_type=F32)
            ST2[j][...] = rows.astype(BF).reshape(4, 4, 16, HALF)
            for d in (2, 1, 3):
                t = (c + d) % 4
                dev = device(j, a, b, t, core)
                go(remote(ST2[j].at[t], RT1[j].at[c], r1t_s.at[j, d], r1t_r.at[j, c], dev))
        back_b(j, par, 0, lambda t: canon(j, SG, (), par, t, c, cols_of(par, j)), ST2[j].at[c])

    def back_b(j, par, d, main, tail):
        a, b, c = axes[j]
        s = (c + d) % 4
        for db in (2, 1, 3):
            t = (b + db) % 4
            dev = device(j, a, t, c, core)
            go(remote(main(t), R2[j][par].at[b, s], r2_s.at[j, par, d, db], r2_r.at[j, par, b, s], dev))
            if par == 0:
                go(remote(tail.at[t], RT2[j].at[b, s], r2t_s.at[j, d, db], r2t_r.at[j, b, s], dev))
        pltpu.make_async_copy(main(b), R2[j][par].at[b, s], l2.at[j, par, d]).start()
        if par == 0:
            pltpu.make_async_copy(tail.at[b], RT2[j].at[b, s], l2t.at[j, d]).start()

    def pass_back(par):
        for d in (1, 3, 2):
            for j in range(3):
                s = (axes[j][2] + d) % 4
                for bl in range(2):
                    got(R1[j][par].at[s, bl], r1_r.at[j, par, s, bl])
                if par == 0:
                    got(RT1[j].at[s], r1t_r.at[j, s])

                def main(t, j=j, s=s):
                    if j == 2:
                        return R1[j][par].at[s, t % 2, :, t // 2]
                    return R1[j][par].at[s, t % 2, t // 2]

                back_b(j, par, d, main, RT1[j].at[s])

    def returned(par, j):
        a, b, c = axes[j]
        for dc in (0, 1, 3, 2):
            s = (c + dc) % 4
            landed(R2[j][par].at[b, s], l2.at[j, par, dc])
            for db in (1, 2, 3):
                t = (b + db) % 4
                got(R2[j][par].at[t, s], r2_r.at[j, par, t, s])

    def tails_returned(j):
        a, b, c = axes[j]
        for dc in (0, 1, 3, 2):
            s = (c + dc) % 4
            landed(RT2[j].at[b, s], l2t.at[j, dc])
            for db in (1, 2, 3):
                t = (b + db) % 4
                got(RT2[j].at[t, s], r2t_r.at[j, t, s])

    def prepare(par, j):
        a, b, c = axes[j]
        left, w = START[par][j] - TAIL_START[j], WIDTH[par][j]
        tails = RT2[j][...].reshape(256, HALF)
        for h in range(2):
            s = 2 * h + (par + b + c) % 2
            pick, low, high = [], [], []
            for k in range(2):
                who = (core + k) % 2
                at = pos[j, s, who][:, None, :]
                row = iota((16, 16, TOK), 1)
                hit = at * 2.0 + who.astype(F32) == row.astype(F32)
                pick.append(jnp.where(hit, 1.0, 0.0).reshape(256, TOK))
                hit = (at == 8.0) & (row == 2 * s + who)
                low.append(jnp.where(hit, 1.0, 0.0).reshape(256, TOK))
                hit = (at == 8.0) & (row == 8 + 2 * s + who)
                high.append(jnp.where(hit, 1.0, 0.0).reshape(256, TOK))
            pick, low, high = (jnp.concatenate(p, axis=1).astype(BF) for p in (pick, low, high))
            PK[j, h] = pick
            both = [over_rows(low, tails), over_rows(high, tails)[:, 2 * HALF - TAIL_WIDTH[j] :]]
            KEEP[j][h, :, :w] = jnp.concatenate(both, axis=1)[:, left : left + w]

    def combine(par, meanwhile):
        swaps = []
        for j in range(3):
            returned(par, j)
            w = WIDTH[par][j]
            for h in range(2):
                total = KEEP[j][h, :, :w] + over_rows(PK[j, h], R2[j][par][:, :, h].reshape(256, w))
                KEEP[j][h, :TOK, :w] = total[:TOK]
                T[j][par][h, 0] = total[TOK:].astype(BF)
                mine, theirs = T[j][par].at[h, 0], T[j][par].at[h, 1]
                cp = remote(mine, theirs, ps_s.at[j, 2 * par + h], ps_r.at[j, 2 * par + h], sib)
                cp.start()
                swaps.append(cp)
        meanwhile()
        for j in range(3):
            a, b, c = axes[j]
            w = WIDTH[par][j]
            for h in range(2):
                s = 2 * h + (par + b + c) % 2
                swaps[2 * j + h].wait_send()
                got(T[j][par].at[h, 1], ps_r.at[j, 2 * par + h])
                total = KEEP[j][h, :TOK, :w] + T[j][par][h, 1].astype(F32)

                @pl.when(s == a)
                def _():
                    OWN[:, cols_of(par, j)] = total

                @pl.when(s != a)
                def _():
                    T[j][par][h, 0] = total.astype(BF)
                    to_line(j, par, h, s).start()

    def to_line(j, par, h, s):
        a, b, c = axes[j]
        dst = T[j][par].at[2 + a // 2, a % 2]
        return remote(T[j][par].at[h, 0], dst, q_s.at[j, 2 * par + h], q_r.at[j, a], device(j, s, b, c, core))

    for j in range(3):
        a, b, c = axes[j]
        landed(metas.at[j, a, core], locm.at[j])
        for s in range(4):
            got(metas.at[j, s, 1 - core], msib_r.at[j, s])
    def complete(j, r):
        landed(T[j][r].at[axes[j][0], core], loc.at[j, r])
        for s in range(4):
            got(T[j][r].at[s, 1 - core], sib_r.at[j, s, r])

    for j in range(3):
        find_slots(j)
        complete(j, 0)
        gather(j, 0, 0)
        depart(j, 0, 0)
    for d in (1, 3):
        rows_across(d, 1)
    second_hop(1)
    pass_on(0, 0)
    rows_across(2, 1)
    for j in range(3):
        complete(j, 1)
        gather(j, 0, 1)
        depart(j, 0, 1)
    for j in range(3):
        gather_tails(j)
        tails_along_b(j)
        tails_along_c(j, 0, ST[j])
    for j in range(3):
        for r in range(2):
            gather(j, 1, r)
    for cp in early:
        cp.wait_send()
    pl.semaphore_signal(done, inc=1, device_id=sib, device_id_type=MESH)
    pass_on(0, 1)
    pass_tails()
    for r in range(2):
        for j in range(3):
            depart(j, 1, r)
    arrive(0, 0)
    arrive(0, 1)
    arrive_tails()
    for i, (src, dst) in enumerate(weights):
        pltpu.make_async_copy(src.at[0], dst, wsem.at[i]).wait()
    forward(0, lambda: pass_on(1, 0))
    pass_on(1, 1)
    old = len(sends)
    pass_back(0)
    arrive(1, 0)
    before_hidden()
    arrive(1, 1)
    forward(1)
    pl.semaphore_wait(done, 1)
    for j in range(3):
        tails_returned(j)
        prepare(0, j)
    combine(0, lambda: lax.fori_loop(0, 2, in_tile, 0))
    for j in range(3):
        prepare(1, j)
    drain(old)
    lax.fori_loop(2, 4, in_tile, 0)
    old = len(sends)
    pass_back(1)
    lax.fori_loop(4, 8, in_tile, 0)
    lax.fori_loop(0, 3, down_tile, 0)
    drain(old)
    combine(1, lambda: drain(len(sends)))
    for m in range(2):

        @pl.when((x + y + z) % 2 == m)
        def _():
            for j in range(3):
                a = axes[j][0]
                total = OWN[:, cols_of(m, j)]
                for d in (1, 3, 2):
                    s = (a + d) % 4
                    part = T[j][m].at[2 + s // 2, s % 2]
                    got(part, q_r.at[j, s])
                    total = total + part[...].astype(F32)
                out[:, cols_of(m, j)] = total.astype(BF)

    for j in range(3):
        a, b, c = axes[j]
        for i in range(4):
            s = 2 * (i % 2) + (i // 2 + b + c) % 2

            @pl.when(s != a)
            def _():
                to_line(j, i // 2, i % 2, s).wait_send()


def run(tokens, out_grad, ids, gates, gate_weight, up_weight, down_weight):
    dma = pltpu.SemaphoreType.DMA
    vm = pltpu.VMEM
    any_spec = pl.BlockSpec(memory_space=pl.ANY)
    vm_spec = pl.BlockSpec(memory_space=pltpu.VMEM)
    shape = jax.ShapeDtypeStruct
    both = [WIDTH[i][j] for j in range(3) for i in range(2)]
    scratch = [vm((4, 2, TOK, w), BF) for w in both]
    scratch += [vm((4, 4, 2, 2, 16, w), BF) for w in both]
    scratch += [vm((4, 4, 2, 16, w), BF) for w in both]
    scratch += [vm((4, 4, 16, w), BF) for w in TAIL_WIDTH] * 2
    scratch += [vm((4, 4, 16, HALF), BF)] * 6
    scratch += [vm((2, 2 * TOK, 768), F32)] * 3
    scratch += [vm((3, 2, 256, 256), BF), vm((TOK, D), F32)]
    scratch += [vm((2, 2, 2, 2, 2, 2, 2, 16, D), BF), vm((2, TAILS, D), BF)]
    scratch += [vm((2, 2, 2, 2, 2, 2, 16, D), BF), vm((TAILS, D), BF)]
    scratch += [vm((ROWS, FF), BF)] * 3
    scratch += [vm((2 * TOP, TOK), F32)] + [vm((3, 4, 2, 16, TOK), F32)] * 2
    scratch += [dma((3, 4, 2))] * 4 + [dma((3, 4))] * 4 + [dma((3, 2)), dma((3,))]
    scratch += [dma((3, 2, 4, 2))] * 2 + [dma((3, 4))] * 2 + [dma((3, 2, 4, 4, 2))] * 2 + [dma((3, 4, 4))] * 2
    scratch += [dma((3, 2, 4, 2)), dma((3, 4))]
    scratch += [dma((3, 2, 4, 2))] * 2 + [dma((3, 4))] * 2 + [dma((3, 2, 4, 4))] * 2 + [dma((3, 4, 4))] * 2
    scratch += [dma((3, 2, 4)), dma((3, 4))]
    scratch += [dma((3, 4))] * 4 + [dma((3,))] + [pltpu.SemaphoreType.REGULAR]
    outs = [vm((TOK, D), BF), vm((1, D, FF), BF), vm((1, D, FF), BF), vm((1, FF, D), BF)]
    outs += [shape((4, 4, 2, 2, 16, w), BF) for w in both]
    outs += [shape((4, 2, 2, 2, 16, w), BF) for w in both]
    outs += [shape((4, 4, 16, w), BF) for w in TAIL_WIDTH] + [shape((4, 4, 16, HALF), BF)] * 3
    return pl.pallas_call(
        kernel,
        name="experts",
        out_shape=outs,
        in_specs=[any_spec] * 2 + [vm_spec] * 2 + [any_spec] * 3,
        out_specs=[vm_spec] * 4 + [any_spec] * 18,
        scratch_shapes=scratch,
        compiler_params=pltpu.CompilerParams(collective_id=0, has_side_effects=True, vmem_limit_bytes=52 << 20),
    )(tokens, out_grad, ids, gates, gate_weight, up_weight, down_weight)[:4]


def body(tokens, out_grad, expert_ids, gates, gate_weight, up_weight, down_weight):
    return tuple(run(tokens, out_grad, expert_ids.T, gates.T, gate_weight, up_weight, down_weight))


def solution(mesh):
    whole = ("node", "local")
    two, three = P(whole, None), P(whole, None, None)
    return jax.shard_map(
        body,
        mesh=mesh,
        in_specs=(two, two, two, two, three, three, three),
        out_specs=(two, three, three, three),
        check_vma=False,
    )
```

```python
import functools

import jax
import jax.numpy as jnp
from jax import lax
from jax.experimental import pallas as pl
from jax.experimental.pallas import tpu as pltpu
from jax.sharding import PartitionSpec as P

MESH = pl.DeviceIdType.MESH
BF, F32 = jnp.bfloat16, jnp.float32
D, FF, TOK, TOP, SLOTS = 2048, 768, 128, 8, 9
WIDTH = ((640, 768, 640), (640, 640, 768))
START = ((0, 640, 1408), (0, 640, 1280))
TAIL_WIDTH = (640, 768, 768)
TAIL_START = (0, 640, 1280)
HALF = 384
ROWS = 1152
MAIN_A, TAILS = 512, 128


def place():
    node, local = lax.axis_index("node"), lax.axis_index("local")
    return local // 2, (node % 8) // 2, (node // 8) * 2 + local % 2, node % 2


def order(j, x, y, z):
    return ((x, y, z), (y, z, x), (z, x, y))[j]


def device(j, a, b, c, core):
    x, y, z = ((a, b, c), (c, a, b), (b, c, a))[j]
    return ((z // 2) * 8 + y * 2 + core, x * 2 + z % 2)


def canon(j, ref, lead, par, b, c, cols):
    q = (par + b + c) % 2
    every = slice(None)
    if j == 0:
        at = (par, c // 2, c % 2, b // 2, b % 2, every)
    elif j == 1:
        at = (par, b // 2, b % 2, every, q, c // 2)
    else:
        at = (par, every, q, c // 2, c % 2, b // 2)
    return ref.at[lead + at + (every, cols)]


def remote(src, dst, ssem, rsem, dev):
    return pltpu.make_async_remote_copy(
        src_ref=src, dst_ref=dst, send_sem=ssem, recv_sem=rsem, device_id=dev, device_id_type=MESH
    )


def greet(partners):
    barrier = pltpu.get_barrier_semaphore()
    for dev in partners:
        pl.semaphore_signal(barrier, inc=1, device_id=dev, device_id_type=MESH)
    pl.semaphore_wait(barrier, len(partners))


def partners_of(x, y, z, core):
    out = [device(0, x, y, z, 1 - core)]
    for d in (1, 2, 3):
        out.append(device(0, (x + d) % 4, y, z, core))
        out.append(device(0, x, (y + d) % 4, z, core))
        out.append(device(0, x, y, (z + d) % 4, core))
    return out


def iota(shape, dim):
    return lax.broadcasted_iota(jnp.int32, shape, dim)


def tail_perm(j, array):
    row, col = iota((128, 256), 0), iota((128, 256), 1)
    core, x, y, z = row % 2, (row // 2) % 4, (row // 8) % 4, row // 32
    a, b, c = order(j, x, y, z)
    want = c * 64 + b * 16 + array * 8 + a * 2 + core
    return (col == want).astype(F32).astype(BF)


def tail_spread(j, half):
    row, col = iota((256, 128), 0), iota((256, 128), 1)
    c, b, h, a, core = row // 64, (row // 16) % 4, (row // 8) % 2, (row // 2) % 4, row % 2
    x, y, z = ((a, b, c), (c, a, b), (b, c, a))[j]
    return ((col == z * 32 + y * 8 + x * 2 + core) & (h == half)).astype(F32).astype(BF)


def over_rows(left, right):
    return lax.dot_general(left, right, (((0,), (0,)), ((), ())), preferred_element_type=F32)


def across(left, right):
    return lax.dot_general(left, right, (((1,), (1,)), ((), ())), preferred_element_type=F32)


def tile(i):
    return pl.ds(pl.multiple_of(i * 256, 256), 256)


def by_two(refs):
    return tuple(refs[2 * j : 2 * j + 2] for j in range(3))


def kernel(tok, grad, ids, gates, gate_w, up_w, down_w, out, gate_out, up_out, down_out, *rest):
    R, R1, RT, RT1, scr = by_two(rest[:6]), by_two(rest[6:12]), rest[12:15], rest[15:18], rest[18:]
    T, S, R2 = (by_two(scr[6 * i : 6 * i + 6]) for i in range(3))
    ST, FT, ST2, RT2, KEEP = (scr[18 + 3 * i : 21 + 3 * i] for i in range(5))
    PK, OWN, XG, XT, SG, SGT, HID, GG, UG, meta, metas, pos = scr[33:45]
    (ag_s, ag_r, sib_s, sib_r, mag_s, mag_r, msib_s, msib_r, loc, locm,
     p2_s, p2_r, p2t_s, p2t_r, p3_s, p3_r, p3t_s, p3t_r, locp, loct,
     r1_s, r1_r, r1t_s, r1t_r, r2_s, r2_r, r2t_s, r2t_r, l2, l2t,
     ps_s, ps_r, q_s, q_r, wsem, done) = scr[45:]
    WG, WU, WD = gate_out.at[0], up_out.at[0], down_out.at[0]
    x, y, z, core = place()
    axes = [order(j, x, y, z) for j in range(3)]
    sib = device(0, x, y, z, 1 - core)
    weights = ((gate_w, WG), (up_w, WU), (down_w, WD))
    for i, (src, dst) in enumerate(weights):
        pltpu.make_async_copy(src.at[0], dst, wsem.at[i]).start()
    meta[:TOP] = ids[...].astype(F32)
    meta[TOP:] = gates[...].astype(F32)
    greet(partners_of(x, y, z, core))
    ins = (tok, grad)
    sends, early = [], []

    def go(cp, kept=sends):
        cp.start()
        kept.append(cp)

    def drain(count):
        for cp in sends[:count]:
            cp.wait_send()
        del sends[:count]

    def got(ref, rsem):
        remote(ref, ref, ag_s.at[0, 0, 0], rsem, sib).wait_recv()

    def landed(ref, sem):
        pltpu.make_async_copy(ref, ref, sem).wait()

    def cols_of(i, j):
        return pl.ds(START[i][j], WIDTH[i][j])

    for j in range(3):
        a, b, c = axes[j]
        for d in (2, 1, 3):
            dev = device(j, (a + d) % 4, b, c, core)
            go(remote(meta, metas.at[j, a, core], mag_s.at[j, d], mag_r.at[j, a], dev))
    def to_lines(r):
        for d in (1, 3):
            for j in range(3):
                a, b, c = axes[j]
                dev = device(j, (a + d) % 4, b, c, core)
                src = ins[r].at[:, cols_of(r, j)]
                go(remote(src, T[j][r].at[a, core], ag_s.at[j, d, r], ag_r.at[j, a, r], dev))

    def metas_across(d):
        for j in range(3):
            s = (axes[j][0] + d) % 4
            m = metas.at[j, s, core]
            got(m, mag_r.at[j, s])
            go(remote(m, m, msib_s.at[j, s], msib_r.at[j, s], sib))

    def rows_across(d, r):
        for j in range(3):
            s = (axes[j][0] + d) % 4
            t = T[j][r].at[s, core]
            got(t, ag_r.at[j, s, r])
            go(remote(t, t, sib_s.at[j, s, r], sib_r.at[j, s, r], sib), early)

    def second_hop(r):
        for j in range(3):
            a, b, c = axes[j]
            way = 1 - 2 * core
            t = T[j][r].at[(a - way) % 4, core]
            dev = device(j, (a + way) % 4, b, c, core)
            go(remote(t, t, ag_s.at[j, 2, r], ag_r.at[j, (a - way) % 4, r], dev), early)

    to_lines(0)
    for j in range(3):
        a, b, c = axes[j]
        go(remote(meta, metas.at[j, a, core], msib_s.at[j, a], msib_r.at[j, a], sib))
        pltpu.make_async_copy(meta, metas.at[j, a, core], locm.at[j]).start()
        for r in range(2):
            src = ins[r].at[:, cols_of(r, j)]
            go(remote(src, T[j][r].at[a, core], sib_s.at[j, a, r], sib_r.at[j, a, r], sib))
            pltpu.make_async_copy(src, T[j][r].at[a, core], loc.at[j, r]).start()
    for d in (1, 3):
        metas_across(d)
        rows_across(d, 0)
    second_hop(0)
    to_lines(1)
    metas_across(2)
    rows_across(2, 0)

    before = (iota((TOK, TOK), 0) < iota((TOK, TOK), 1)).astype(F32).astype(BF)

    def one_hot(j, s, gate, last):
        a = axes[j][0]
        e = iota((16, 1), 0)
        dev = device(j, a, e // 4, e % 4, core)
        expert = (dev[0] * 8 + dev[1]).astype(F32)
        parts = []
        for k in range(2):
            info = metas[j, s, k]
            value = jnp.ones((16, TOK), F32)
            if gate:
                value = jnp.zeros((16, TOK), F32)
                for i in range(TOP):
                    hit = info[i : i + 1, :] == expert
                    value = value + jnp.where(hit, info[TOP + i : TOP + i + 1, :], 0.0)
            at = pos[j, s, k][:, None, :]
            if last:
                hit = (at == 8.0) & (iota((16, 8, TOK), 1) == 2 * s + k)
            else:
                hit = at * 2.0 + k == iota((16, 16, TOK), 1).astype(F32)
            parts.append(jnp.where(hit, value[:, None, :], 0.0).reshape(128 if last else 256, TOK))
        return jnp.concatenate(parts, axis=1).astype(BF)

    def find_slots(j):
        a = axes[j][0]
        e = iota((16, 1), 0)
        dev = device(j, a, e // 4, e % 4, core)
        expert = (dev[0] * 8 + dev[1]).astype(F32)
        for s in range(4):
            for k in range(2):
                info = metas[j, s, k]
                named = jnp.zeros((16, TOK), F32)
                for i in range(TOP):
                    named = named + jnp.where(info[i : i + 1, :] == expert, 1.0, 0.0)
                earlier = jnp.dot(named.astype(BF), before, preferred_element_type=F32)
                pos[j, s, k] = jnp.where(named > 0.5, earlier, -1.0)

    def gather(j, par, r):
        a, b, c = axes[j]
        w = WIDTH[r][j]
        for h in range(2):
            s = 2 * h + (par + b + c) % 2
            rows = T[j][r][s].reshape(2 * TOK, w)
            main = jnp.dot(one_hot(j, s, r == 1, False), rows, preferred_element_type=F32)
            S[j][r][:, :, par, h] = main.astype(BF).reshape(4, 4, 16, w)

    def gather_tails(j):
        tails = []
        for r in range(2):
            w = WIDTH[r][j]
            rows = jnp.zeros((TAILS, w), F32)
            for s in range(4):
                picked = T[j][r][s].reshape(2 * TOK, w)
                rows = rows + jnp.dot(one_hot(j, s, r == 1, True), picked, preferred_element_type=F32)
            left = START[r][j] - TAIL_START[j]
            right = TAIL_WIDTH[j] - w - left
            rows = [rows]
            if left:
                rows = [jnp.zeros((TAILS, left), F32)] + rows
            if right:
                rows = rows + [jnp.zeros((TAILS, right), F32)]
            tails.append(jnp.concatenate(rows, axis=1).reshape(16, 8, TAIL_WIDTH[j]))
        ST[j][...] = jnp.concatenate(tails, axis=1).astype(BF).reshape(4, 4, 16, TAIL_WIDTH[j])

    def along_b(j, par, r):
        a, b, c = axes[j]
        for d in (2, 1, 3):
            t = (b + d) % 4
            dev = device(j, a, t, c, core)
            src, dst = S[j][r].at[t, :, par], R[j][r].at[b, :, par]
            go(remote(src, dst, p2_s.at[j, par, d, r], p2_r.at[j, par, b, r], dev))

    def along_c(j, par, d, r, main):
        a, b, c = axes[j]
        s = (b + d) % 4
        dst = canon(j, XG, (r,), par, s, c, cols_of(r, j))
        for dc in (2, 1, 3):
            t = (c + dc) % 4
            dev = device(j, a, b, t, core)
            go(remote(main.at[s, t, par], dst, p3_s.at[j, par, d, dc, r], p3_r.at[j, par, c, s, r], dev))
        pltpu.make_async_copy(main.at[s, c, par], dst, locp.at[j, par, d, r]).start()

    def depart(j, par, r):
        along_b(j, par, r)
        along_c(j, par, 0, r, S[j][r])

    def tails_along_b(j):
        a, b, c = axes[j]
        for d in (2, 1, 3):
            t = (b + d) % 4
            dev = device(j, a, t, c, core)
            go(remote(ST[j].at[t], RT[j].at[b], p2t_s.at[j, d], p2t_r.at[j, b], dev))

    def tails_along_c(j, d, tail):
        a, b, c = axes[j]
        s = (b + d) % 4
        for dc in (2, 1, 3):
            t = (c + dc) % 4
            dev = device(j, a, b, t, core)
            go(remote(tail.at[s, t], FT[j].at[c, s], p3t_s.at[j, d, dc], p3t_r.at[j, c, s], dev))
        pltpu.make_async_copy(tail.at[s, c], FT[j].at[c, s], loct.at[j, d]).start()

    def pass_on(par, r):
        for d in (1, 3, 2):
            for j in range(3):
                s = (axes[j][1] + d) % 4
                got(R[j][r].at[s, :, par], p2_r.at[j, par, s, r])
                along_c(j, par, d, r, R[j][r])

    def pass_tails():
        for d in (1, 3, 2):
            for j in range(3):
                s = (axes[j][1] + d) % 4
                got(RT[j].at[s], p2t_r.at[j, s])
                tails_along_c(j, d, RT[j])

    def arrive(par, r):
        for j in range(3):
            a, b, c = axes[j]
            for db in (0, 1, 3, 2):
                s = (b + db) % 4
                landed(canon(j, XG, (r,), par, s, c, cols_of(r, j)), locp.at[j, par, db, r])
                for dc in (1, 2, 3):
                    t = (c + dc) % 4
                    got(canon(j, XG, (r,), par, s, t, cols_of(r, j)), p3_r.at[j, par, t, s, r])

    def arrive_tails():
        for j in range(3):
            a, b, c = axes[j]
            for db in range(4):
                s = (b + db) % 4
                landed(FT[j].at[c, s], loct.at[j, db])
                for dc in (1, 2, 3):
                    t = (c + dc) % 4
                    got(FT[j].at[t, s], p3t_r.at[j, t, s])
            rows = FT[j][...].reshape(256, TAIL_WIDTH[j])
            for r in range(2):
                picked = jnp.dot(tail_perm(j, r), rows, preferred_element_type=F32).astype(BF)
                left = START[r][j] - TAIL_START[j]
                XT[r, :, cols_of(r, j)] = picked[:, left : left + WIDTH[r][j]]

    first, size = (0, MAIN_A + TAILS), (MAIN_A + TAILS, MAIN_A)

    def rows_of(r, par):
        main = XG[r, par].reshape(MAIN_A, D)
        return jnp.concatenate([main, XT[r]], axis=0) if par == 0 else main

    def before_hidden():
        def tile_of(i, carry):
            cols = tile(i)
            rows = rows_of(0, 1)
            KEEP[0][:, :, cols] = jnp.dot(rows, WG[:, cols], preferred_element_type=F32).reshape(2, 256, 256)
            KEEP[1][:, :, cols] = jnp.dot(rows, WU[:, cols], preferred_element_type=F32).reshape(2, 256, 256)
            return carry

        lax.fori_loop(0, FF // 256, tile_of, 0)

    def forward(par, meanwhile=lambda: None, later=lambda: None):
        span = pl.ds(first[par], size[par])

        def hidden_tile(i, carry):
            cols = tile(i)
            if par == 0:
                rows = rows_of(0, par)
                gate_pre = jnp.dot(rows, WG[:, cols], preferred_element_type=F32)
                up_pre = jnp.dot(rows, WU[:, cols], preferred_element_type=F32)
            else:
                gate_pre = KEEP[0][:, :, cols].reshape(MAIN_A, 256)
                up_pre = KEEP[1][:, :, cols].reshape(MAIN_A, 256)
            hidden_grad = across(rows_of(1, par), WD[cols, :])
            logistic = jax.nn.sigmoid(gate_pre)
            silu_gate = gate_pre * logistic
            HID[span, cols] = (silu_gate * up_pre).astype(BF)
            UG[span, cols] = (hidden_grad * silu_gate).astype(BF)
            GG[span, cols] = (hidden_grad * up_pre * logistic * (1.0 + gate_pre * (1.0 - logistic))).astype(BF)
            return carry

        lax.fori_loop(0, FF // 256, hidden_tile, 0)
        meanwhile()

        def slot_tile(i, carry):
            cols = tile(i)
            rows = (across(GG[span, :], WG[cols, :]) + across(UG[span, :], WU[cols, :])).astype(BF)
            SG[par, :, :, :, :, :, :, cols] = rows[:MAIN_A].reshape(2, 2, 2, 2, 2, 16, 256)
            if par == 0:
                SGT[:, cols] = rows[MAIN_A:]
            return carry

        ready = 0
        for j in range(3):
            stop = -(-(START[par][j] + WIDTH[par][j]) // 256)
            lax.fori_loop(ready, stop, slot_tile, 0)
            ready = stop
            back_c(par, j)
            if j == 0:
                later()

    def in_tile(i, carry):
        cols = tile(i)
        parts = [XG[0, 0, :, :, :, :, :, :, cols].reshape(MAIN_A, 256), XT[0, :, cols]]
        rows = jnp.concatenate(parts + [XG[0, 1, :, :, :, :, :, :, cols].reshape(MAIN_A, 256)], axis=0)
        WG[cols, :] = over_rows(rows, GG[...]).astype(BF)
        WU[cols, :] = over_rows(rows, UG[...]).astype(BF)
        return carry

    def down_tile(i, carry):
        cols = tile(i)
        rows = jnp.concatenate([rows_of(1, 0), rows_of(1, 1)], axis=0)
        WD[cols, :] = over_rows(HID[:, cols], rows).astype(BF)
        return carry

    def back_c(par, j):
        a, b, c = axes[j]
        for d in (2, 1, 3):
            t = (c + d) % 4
            dev = device(j, a, b, t, core)
            for bl in range(2):
                if j == 0:
                    at = (par, t // 2, t % 2, slice(None), bl, slice(None))
                elif j == 1:
                    at = (par, slice(None), bl, slice(None), (par + bl + t) % 2, t // 2)
                else:
                    at = (par, slice(None), (par + bl + t) % 2, t // 2, t % 2, slice(None))
                src = SG.at[at + (slice(None), cols_of(par, j))]
                go(remote(src, R1[j][par].at[c, bl], r1_s.at[j, par, d, bl], r1_r.at[j, par, c, bl], dev))
        if par == 0:
            lo, hi = TAIL_START[j], TAIL_START[j] + TAIL_WIDTH[j] - HALF
            rows = jnp.dot(tail_spread(j, 0), SGT[:, lo : lo + HALF], preferred_element_type=F32)
            rows = rows + jnp.dot(tail_spread(j, 1), SGT[:, hi : hi + HALF], preferred_element_type=F32)
            ST2[j][...] = rows.astype(BF).reshape(4, 4, 16, HALF)
            for d in (2, 1, 3):
                t = (c + d) % 4
                dev = device(j, a, b, t, core)
                go(remote(ST2[j].at[t], RT1[j].at[c], r1t_s.at[j, d], r1t_r.at[j, c], dev))
        back_b(j, par, 0, lambda t: canon(j, SG, (), par, t, c, cols_of(par, j)), ST2[j].at[c])

    def back_b(j, par, d, main, tail):
        a, b, c = axes[j]
        s = (c + d) % 4
        for db in (2, 1, 3):
            t = (b + db) % 4
            dev = device(j, a, t, c, core)
            go(remote(main(t), R2[j][par].at[b, s], r2_s.at[j, par, d, db], r2_r.at[j, par, b, s], dev))
            if par == 0:
                go(remote(tail.at[t], RT2[j].at[b, s], r2t_s.at[j, d, db], r2t_r.at[j, b, s], dev))
        pltpu.make_async_copy(main(b), R2[j][par].at[b, s], l2.at[j, par, d]).start()
        if par == 0:
            pltpu.make_async_copy(tail.at[b], RT2[j].at[b, s], l2t.at[j, d]).start()

    def pass_back(par):
        for d in (1, 3, 2):
            for j in range(3):
                s = (axes[j][2] + d) % 4
                for bl in range(2):
                    got(R1[j][par].at[s, bl], r1_r.at[j, par, s, bl])
                if par == 0:
                    got(RT1[j].at[s], r1t_r.at[j, s])

                def main(t, j=j, s=s):
                    if j == 2:
                        return R1[j][par].at[s, t % 2, :, t // 2]
                    return R1[j][par].at[s, t % 2, t // 2]

                back_b(j, par, d, main, RT1[j].at[s])

    def returned(par, j):
        a, b, c = axes[j]
        for dc in (0, 1, 3, 2):
            s = (c + dc) % 4
            landed(R2[j][par].at[b, s], l2.at[j, par, dc])
            for db in (1, 2, 3):
                t = (b + db) % 4
                got(R2[j][par].at[t, s], r2_r.at[j, par, t, s])

    def tails_returned(j):
        a, b, c = axes[j]
        for dc in (0, 1, 3, 2):
            s = (c + dc) % 4
            landed(RT2[j].at[b, s], l2t.at[j, dc])
            for db in (1, 2, 3):
                t = (b + db) % 4
                got(RT2[j].at[t, s], r2t_r.at[j, t, s])

    def prepare(par, j):
        a, b, c = axes[j]
        left, w = START[par][j] - TAIL_START[j], WIDTH[par][j]
        tails = RT2[j][...].reshape(256, HALF)
        for h in range(2):
            s = 2 * h + (par + b + c) % 2
            pick, low, high = [], [], []
            for k in range(2):
                who = (core + k) % 2
                at = pos[j, s, who][:, None, :]
                row = iota((16, 16, TOK), 1)
                hit = at * 2.0 + who.astype(F32) == row.astype(F32)
                pick.append(jnp.where(hit, 1.0, 0.0).reshape(256, TOK))
                hit = (at == 8.0) & (row == 2 * s + who)
                low.append(jnp.where(hit, 1.0, 0.0).reshape(256, TOK))
                hit = (at == 8.0) & (row == 8 + 2 * s + who)
                high.append(jnp.where(hit, 1.0, 0.0).reshape(256, TOK))
            pick, low, high = (jnp.concatenate(p, axis=1).astype(BF) for p in (pick, low, high))
            PK[j, h] = pick
            both = [over_rows(low, tails), over_rows(high, tails)[:, 2 * HALF - TAIL_WIDTH[j] :]]
            KEEP[j][h, :, :w] = jnp.concatenate(both, axis=1)[:, left : left + w]

    def combine(par, meanwhile):
        swaps = []
        for j in range(3):
            returned(par, j)
            w = WIDTH[par][j]
            for h in range(2):
                total = KEEP[j][h, :, :w] + over_rows(PK[j, h], R2[j][par][:, :, h].reshape(256, w))
                KEEP[j][h, :TOK, :w] = total[:TOK]
                T[j][par][h, 0] = total[TOK:].astype(BF)
                mine, theirs = T[j][par].at[h, 0], T[j][par].at[h, 1]
                cp = remote(mine, theirs, ps_s.at[j, 2 * par + h], ps_r.at[j, 2 * par + h], sib)
                cp.start()
                swaps.append(cp)
        meanwhile()
        for j in range(3):
            a, b, c = axes[j]
            w = WIDTH[par][j]
            for h in range(2):
                s = 2 * h + (par + b + c) % 2
                swaps[2 * j + h].wait_send()
                got(T[j][par].at[h, 1], ps_r.at[j, 2 * par + h])
                total = KEEP[j][h, :TOK, :w] + T[j][par][h, 1].astype(F32)

                @pl.when(s == a)
                def _():
                    OWN[:, cols_of(par, j)] = total

                @pl.when(s != a)
                def _():
                    T[j][par][h, 0] = total.astype(BF)
                    to_line(j, par, h, s).start()

    def to_line(j, par, h, s):
        a, b, c = axes[j]
        dst = T[j][par].at[2 + a // 2, a % 2]
        return remote(T[j][par].at[h, 0], dst, q_s.at[j, 2 * par + h], q_r.at[j, a], device(j, s, b, c, core))

    for j in range(3):
        a, b, c = axes[j]
        landed(metas.at[j, a, core], locm.at[j])
        for s in range(4):
            got(metas.at[j, s, 1 - core], msib_r.at[j, s])
    def complete(j, r):
        landed(T[j][r].at[axes[j][0], core], loc.at[j, r])
        for s in range(4):
            got(T[j][r].at[s, 1 - core], sib_r.at[j, s, r])

    for j in range(3):
        find_slots(j)
        complete(j, 0)
        gather(j, 0, 0)
        depart(j, 0, 0)
    for d in (1, 3):
        rows_across(d, 1)
    second_hop(1)
    pass_on(0, 0)
    rows_across(2, 1)
    for j in range(3):
        complete(j, 1)
        gather(j, 0, 1)
        depart(j, 0, 1)
    for j in range(3):
        gather_tails(j)
        tails_along_b(j)
        tails_along_c(j, 0, ST[j])
    for j in range(3):
        for r in range(2):
            gather(j, 1, r)
    for cp in early:
        cp.wait_send()
    pl.semaphore_signal(done, inc=1, device_id=sib, device_id_type=MESH)
    pass_on(0, 1)
    pass_tails()
    for r in range(2):
        for j in range(3):
            depart(j, 1, r)
    arrive(0, 0)
    arrive(0, 1)
    arrive_tails()
    for i, (src, dst) in enumerate(weights):
        pltpu.make_async_copy(src.at[0], dst, wsem.at[i]).wait()
    forward(0, lambda: pass_on(1, 0), lambda: pass_on(1, 1))
    old = len(sends)
    pass_back(0)
    arrive(1, 0)
    before_hidden()
    arrive(1, 1)
    forward(1)
    pl.semaphore_wait(done, 1)
    for j in range(3):
        tails_returned(j)
        prepare(0, j)
    combine(0, lambda: lax.fori_loop(0, 2, in_tile, 0))
    for j in range(3):
        prepare(1, j)
    drain(old)
    lax.fori_loop(2, 4, in_tile, 0)
    old = len(sends)
    pass_back(1)
    lax.fori_loop(4, 8, in_tile, 0)
    lax.fori_loop(0, 3, down_tile, 0)
    drain(old)
    combine(1, lambda: drain(len(sends)))
    for m in range(2):

        @pl.when((x + y + z) % 2 == m)
        def _():
            for j in range(3):
                a = axes[j][0]
                total = OWN[:, cols_of(m, j)]
                for d in (1, 3, 2):
                    s = (a + d) % 4
                    part = T[j][m].at[2 + s // 2, s % 2]
                    got(part, q_r.at[j, s])
                    total = total + part[...].astype(F32)
                out[:, cols_of(m, j)] = total.astype(BF)

    for j in range(3):
        a, b, c = axes[j]
        for i in range(4):
            s = 2 * (i % 2) + (i // 2 + b + c) % 2

            @pl.when(s != a)
            def _():
                to_line(j, i // 2, i % 2, s).wait_send()


def run(tokens, out_grad, ids, gates, gate_weight, up_weight, down_weight):
    dma = pltpu.SemaphoreType.DMA
    vm = pltpu.VMEM
    any_spec = pl.BlockSpec(memory_space=pl.ANY)
    vm_spec = pl.BlockSpec(memory_space=pltpu.VMEM)
    shape = jax.ShapeDtypeStruct
    both = [WIDTH[i][j] for j in range(3) for i in range(2)]
    scratch = [vm((4, 2, TOK, w), BF) for w in both]
    scratch += [vm((4, 4, 2, 2, 16, w), BF) for w in both]
    scratch += [vm((4, 4, 2, 16, w), BF) for w in both]
    scratch += [vm((4, 4, 16, w), BF) for w in TAIL_WIDTH] * 2
    scratch += [vm((4, 4, 16, HALF), BF)] * 6
    scratch += [vm((2, 2 * TOK, 768), F32)] * 3
    scratch += [vm((3, 2, 256, 256), BF), vm((TOK, D), F32)]
    scratch += [vm((2, 2, 2, 2, 2, 2, 2, 16, D), BF), vm((2, TAILS, D), BF)]
    scratch += [vm((2, 2, 2, 2, 2, 2, 16, D), BF), vm((TAILS, D), BF)]
    scratch += [vm((ROWS, FF), BF)] * 3
    scratch += [vm((2 * TOP, TOK), F32)] + [vm((3, 4, 2, 16, TOK), F32)] * 2
    scratch += [dma((3, 4, 2))] * 4 + [dma((3, 4))] * 4 + [dma((3, 2)), dma((3,))]
    scratch += [dma((3, 2, 4, 2))] * 2 + [dma((3, 4))] * 2 + [dma((3, 2, 4, 4, 2))] * 2 + [dma((3, 4, 4))] * 2
    scratch += [dma((3, 2, 4, 2)), dma((3, 4))]
    scratch += [dma((3, 2, 4, 2))] * 2 + [dma((3, 4))] * 2 + [dma((3, 2, 4, 4))] * 2 + [dma((3, 4, 4))] * 2
    scratch += [dma((3, 2, 4)), dma((3, 4))]
    scratch += [dma((3, 4))] * 4 + [dma((3,))] + [pltpu.SemaphoreType.REGULAR]
    outs = [vm((TOK, D), BF), vm((1, D, FF), BF), vm((1, D, FF), BF), vm((1, FF, D), BF)]
    outs += [shape((4, 4, 2, 2, 16, w), BF) for w in both]
    outs += [shape((4, 2, 2, 2, 16, w), BF) for w in both]
    outs += [shape((4, 4, 16, w), BF) for w in TAIL_WIDTH] + [shape((4, 4, 16, HALF), BF)] * 3
    return pl.pallas_call(
        kernel,
        name="experts",
        out_shape=outs,
        in_specs=[any_spec] * 2 + [vm_spec] * 2 + [any_spec] * 3,
        out_specs=[vm_spec] * 4 + [any_spec] * 18,
        scratch_shapes=scratch,
        compiler_params=pltpu.CompilerParams(collective_id=0, has_side_effects=True, vmem_limit_bytes=52 << 20),
    )(tokens, out_grad, ids, gates, gate_weight, up_weight, down_weight)[:4]


def body(tokens, out_grad, expert_ids, gates, gate_weight, up_weight, down_weight):
    return tuple(run(tokens, out_grad, expert_ids.T, gates.T, gate_weight, up_weight, down_weight))


def solution(mesh):
    whole = ("node", "local")
    two, three = P(whole, None), P(whole, None, None)
    return jax.shard_map(
        body,
        mesh=mesh,
        in_specs=(two, two, two, two, three, three, three),
        out_specs=(two, three, three, three),
        check_vma=False,
    )
```
